512 devices in a mesh: ka: 8 (over z_lo), atoms: 64 (over y, z_hi, x, core).
Axes of the slice: x: 4, y: 4, z: 16 (z_hi: 2, z_lo: 8; z = z_hi * 8 + z_lo), core: 2. Of those that a mesh axis runs over, the one named last changes fastest.
Arguments:
- positions: float32 [3, 262144], P(None, ('ka', 'atoms')), may hold values from 0 to 1
- charges: float32 [8, 262144], P(None, ('ka', 'atoms')), may hold values from -6 to 6
- miller: int32 [3, 4096], P(None, 'ka'), may hold values from -10 to 10, as said below
Outputs:
- energies: float32 [262144], P(('ka', 'atoms'))
- forces: float32 [3, 262144], P(None, ('ka', 'atoms'))
The draws below stay inside these ranges and needn't reach their ends.
Inputs may be any that keep to these rules, and one draw needn't show every extreme that they name: `miller`: the columns are distinct nonzero triples.
All inputs are finite; a program needn't handle non-finite values.
Results may differ from the reference program's by a relative error of at most 0.0003.
Values sent between devices are 32-bit elements; how exact they have to be, the bound alone decides.
No kernel may reach another device: no remote copies, remote signals or barrier semaphores. Data moves between devices by JAX's collectives and lax.ppermute only.
A program may use at most 64 MiB of HBM per device.

```python
import jax
import jax.numpy as jnp
from jax import lax

LATENT = 8
K = 4096
ATOM_DEV = 512
ATOMS = 262144


def draw_miller(key, part):
    key = jax.random.fold_in(key, 5)
    picked = jax.random.permutation(key, 9260)[:K]
    picked = picked + (picked >= 4630).astype(jnp.int32)
    first = picked // 441 - 10
    second = picked // 21 % 21 - 10
    third = picked % 21 - 10
    return jnp.stack([first, second, third]).astype(jnp.int32)


def steps_of(stream_key, dims, shards, low, high):
    factor_of = 1.0
    for dim, blocks in shards:
        draws = jax.random.uniform(jax.random.fold_in(jax.random.fold_in(stream_key, 6), dim), (blocks,), jnp.float32, low / len(shards), high / len(shards))
        factor_of = factor_of * jnp.repeat(jnp.exp(draws), dims[dim] // blocks).reshape((-1,) + (1,) * (len(dims) - 1 - dim))
    return factor_of


def noise(own_key, shape, deviation, reach, cuts=(), held_as=jnp.bfloat16):
    drawn = deviation * jax.random.normal(own_key, shape, jnp.float32)
    if cuts:
        drawn = drawn * steps_of(own_key, shape, cuts, -0.22, 0.18)
    return jnp.clip(drawn, -reach, reach).astype(held_as)


def setup_inputs(seed: int = 0) -> dict:
    key_list = jax.random.split(jax.random.key(seed), 4)
    return {
        "positions": jnp.clip(1.0 * jax.random.uniform(key_list[0], (3, ATOMS), jnp.float32) ** steps_of(key_list[0], (3, ATOMS), ((1, 512),), -0.2, 0.2), 0.0, 1.0),
        "charges": noise(key_list[1], (LATENT, ATOMS), 1.0, 6.0, ((1, 512),), jnp.float32),
        "miller": draw_miller(jax.random.fold_in(key_list[3], 71), 0),
    }


def phase_tiles(miller_f, pos):
    angle = 2.0 * jnp.pi * jnp.dot(miller_f.T, pos, precision=lax.Precision.HIGHEST, preferred_element_type=jnp.float32)
    return (jnp.cos(angle), jnp.sin(angle))

def reference(positions, charges, miller):
    miller_f = miller.astype(jnp.float32)
    blocks = ATOMS // ATOM_DEV
    pos_blocks = positions.reshape(3, blocks, ATOM_DEV).transpose(1, 0, 2)
    chg_blocks = charges.reshape(LATENT, blocks, ATOM_DEV).transpose(1, 0, 2)

    def accumulate(total, item):
        pos, chg = item
        cosines, sines = phase_tiles(miller_f, pos)
        real_part = jnp.dot(cosines, chg.T, precision=lax.Precision.HIGHEST, preferred_element_type=jnp.float32)
        imag_part = jnp.dot(sines, chg.T, precision=lax.Precision.HIGHEST, preferred_element_type=jnp.float32)
        return (total + jnp.concatenate([real_part, imag_part], axis=1), None)
    start = jnp.zeros((K, 2 * LATENT), jnp.float32)
    struct, unused = lax.scan(accumulate, start, (pos_blocks, chg_blocks))
    struct = struct / jnp.sqrt(jnp.float32(ATOMS))
    msq = lax.optimization_barrier(jnp.sum(miller_f * miller_f, axis=0))
    weight = jnp.exp(-0.025 * msq) / msq
    real_w = weight[:, None] * struct[:, :LATENT]
    imag_w = weight[:, None] * struct[:, LATENT:]
    left_cos = jnp.concatenate([real_w] + [-miller_f[d][:, None] * imag_w for d in range(3)], axis=1)
    left_sin = jnp.concatenate([imag_w] + [miller_f[d][:, None] * real_w for d in range(3)], axis=1)

    def per_block(item):
        pos, chg = item
        cosines, sines = phase_tiles(miller_f, pos)
        total = jnp.dot(left_cos.T, cosines, precision=lax.Precision.HIGHEST, preferred_element_type=jnp.float32)
        total = total + jnp.dot(left_sin.T, sines, precision=lax.Precision.HIGHEST, preferred_element_type=jnp.float32)
        energy = 0.25 * lax.optimization_barrier(jnp.sum(chg * total[:LATENT], axis=0))
        force = jnp.stack([0.1 * lax.optimization_barrier(jnp.sum(chg * total[LATENT * (d + 1):LATENT * (d + 2)], axis=0)) for d in range(3)])
        return (energy, force)
    energy_b, force_b = lax.map(per_block, (pos_blocks, chg_blocks))
    energies = energy_b.reshape(ATOMS)
    forces = force_b.transpose(1, 0, 2).reshape(3, ATOMS)
    return (energies, forces)
```

```python
import functools

import jax
import jax.numpy as jnp
from jax import lax
from jax.experimental import pallas as pl
from jax.experimental.pallas import tpu as pltpu
from jax.sharding import Mesh
from jax.sharding import PartitionSpec as P

TOP = 10
LATENT = 8
TILES = 32
ROWS = 8
HALF = 176
LANES = 384
COUNT_LANE = 352
SIN = (3.141592640130706, -5.167710083507839, 2.550077523214083, -0.5982912856178239, 0.07765766030006041)
COS = (
    1.0,
    -4.934802137078852,
    4.058709159556494,
    -1.3352120030499017,
    0.23493731380758293,
    -0.02439632432974524,
)
F32 = jnp.float32
BF16 = jnp.bfloat16
SPREAD = ("y", "x", "c")
COLUMN = ("zl", "zh")


def horner(coefs, u):
    out = jnp.full_like(u, coefs[-1])
    for c in coefs[-2::-1]:
        out = out * u + c
    return out


def orders(shape):
    r = lax.broadcasted_iota(jnp.int32, shape, 0)
    late = jnp.where(r == 9, 9, jnp.where(r == 10, 10, jnp.where(r == 11, -9, jnp.where(r == 12, -10, 0))))
    return jnp.where(r < 8, r + 1, late).astype(F32)


def table(coordinate):
    t = orders((16, coordinate.shape[1])) * coordinate
    t = t - jnp.round(t)
    u = t * t
    s = t * horner(SIN, u)
    c = horner(COS, u)
    return 1.0 - 2.0 * s * s, 2.0 * s * c


def row_of(n):
    n = abs(n)
    return n - 1 if 1 <= n <= 8 else (8 if n == 0 else n)


def split(x):
    high = x.astype(BF16)
    return high, (x - high.astype(F32)).astype(BF16)


def pair_tile(tile, cx, sx, cy, sy):
    if tile < 21:
        b = tile - TOP
        r = row_of(b)
        ca, sa, cb, sb = cx[0:8], sx[0:8], cy[r : r + 1], sy[r : r + 1]
        minus = b < 0
    elif tile < 30:
        i, j = divmod(tile - 21, 3)
        r = 8 + i
        ca, sa = cx[r : r + 1], sx[r : r + 1]
        rows = slice(8, 16) if j == 2 else slice(0, 8)
        cb, sb = cy[rows], sy[rows]
        minus = j == 1
    else:
        zero = jnp.zeros((8, cx.shape[1]), F32)
        return zero, zero
    cc, ss, sc, cs = ca * cb, sa * sb, sa * cb, ca * sb
    if minus:
        return cc + ss, sc - cs
    return cc - ss, sc + cs


def z_rows(rows, charges):
    return [rows[row_of(n) : row_of(n) + 1] * charges for n in range(TOP + 1)]


def nt(a, b):
    return lax.dot_general(a, b, (((1,), (1,)), ((), ())), preferred_element_type=F32)


def nn(a, b):
    return jnp.dot(a, b, preferred_element_type=F32)


def product(mul, a, b):
    return mul(a[0], b[0]) + (mul(a[0], b[1]) + mul(a[1], b[0]))


def struct_kernel(pos_ref, chg_ref, out_ref, re_hi, re_lo, im_hi, im_lo):
    charges = chg_ref[...]
    atoms = charges.shape[1]
    cx, sx = table(pos_ref[0:1, :])
    cy, sy = table(pos_ref[1:2, :])
    cz, sz = table(pos_ref[2:3, :])
    for two in range(TILES // 2):
        first = pair_tile(2 * two, cx, sx, cy, sy)
        second = pair_tile(2 * two + 1, cx, sx, cy, sy)
        rows = slice(16 * two, 16 * two + 16)
        re_hi[rows, :], re_lo[rows, :] = split(jnp.concatenate([first[0], second[0]], axis=0))
        im_hi[rows, :], im_lo[rows, :] = split(jnp.concatenate([first[1], second[1]], axis=0))
    cq = z_rows(cz, charges)
    sq = z_rows(sz, charges)
    blank = lambda n: [jnp.zeros((n, atoms), F32)]
    real = product(nt, (re_hi[...], re_lo[...]), split(jnp.concatenate(cq + sq + blank(80), axis=0)))
    imag = product(nt, (im_hi[...], im_lo[...]), split(jnp.concatenate(blank(48) + sq + cq + blank(32), axis=0)))
    out_ref[:, :, 0:128] = real[:, 0:128].reshape(TILES, ROWS, 128)
    out_ref[:, :, 128:256] = (real[:, 128:256] + imag[:, 0:128]).reshape(TILES, ROWS, 128)
    out_ref[:, :, 256:384] = imag[:, 128:256].reshape(TILES, ROWS, 128)


def slot_of(a, b):
    ordinary = (a >= 1) & (a <= 8)
    i = jnp.where(a == 9, 1, jnp.where(a == 10, 2, 0))
    up = (b >= 1) & (b <= 8)
    down = (b <= -1) & (b >= -8)
    j = jnp.where(up, 0, jnp.where(down, 1, 2))
    rest = jnp.where(b == 9, 1, jnp.where(b == 10, 2, jnp.where(b == -9, 3, jnp.where(b == -10, 4, 0))))
    row = jnp.where(up, b - 1, jnp.where(down, -b - 1, rest))
    return jnp.where(ordinary, (b + TOP) * 8 + a - 1, (21 + i * 3 + j) * 8 + row)


def collect_kernel(tile_ref, part_ref, miller_ref, out_ref):
    total = jnp.sum(part_ref[...], axis=0)
    a, b, c = miller_ref[0:1, :], miller_ref[1:2, :], miller_ref[2:3, :]
    sign = jnp.where(a < 0, -1, 1)
    a, b, c = a * sign, b * sign, c * sign
    listed = a.shape[1]
    slot = slot_of(a, b) - tile_ref[0] * 8
    pair = (slot == lax.broadcasted_iota(jnp.int32, (ROWS, listed), 0)).astype(F32)
    place = c + (TOP + COUNT_LANE - 256)
    third = (place == lax.broadcasted_iota(jnp.int32, (128, listed), 0)).astype(F32)
    counts = nt(pair.astype(BF16), third.astype(BF16))
    out_ref[:, :, 0:256] = jnp.broadcast_to(total[:, 0:256], (out_ref.shape[0], ROWS, 256))
    out_ref[:, :, 256:384] = jnp.broadcast_to(total[:, 256:384] + counts, (out_ref.shape[0], ROWS, 128))


def weigh_kernel(scale, copies, tile_ref, part_ref, out_ref):
    total = jnp.sum(part_ref[...], axis=0)
    tile = tile_ref[0]
    row = lax.broadcasted_iota(jnp.int32, (ROWS, LANES), 0)
    lane = lax.broadcasted_iota(jnp.int32, (ROWS, LANES), 1)
    inner = jnp.where(lane >= HALF, lane - HALF, lane)
    second = inner >= HALF // 2
    c = jnp.where(second, inner - HALF // 2, inner) >> 3
    late = tile - 21
    i = jnp.where(late >= 6, 2, jnp.where(late >= 3, 1, 0))
    j = late - 3 * i
    late_a = jnp.where(i == 2, 10, jnp.where(i == 1, 9, 0))
    rest = jnp.where(row == 1, 9, jnp.where(row == 2, 10, jnp.where(row == 3, -9, jnp.where(row == 4, -10, 0))))
    late_b = jnp.where(j == 0, row + 1, jnp.where(j == 1, -row - 1, rest))
    a = jnp.where(tile < 21, row + 1, late_a)
    b = jnp.where(tile < 21, tile - TOP, late_b)
    square = jnp.maximum(a * a + b * b + c * c, 1).astype(F32)
    weight = jnp.exp(-0.025 * square) / square * scale
    wide_lane = lax.broadcasted_iota(jnp.int32, (128, LANES), 1)
    wide_inner = jnp.where(wide_lane >= HALF, wide_lane - HALF, wide_lane)
    wide_c = jnp.where(wide_inner >= HALF // 2, wide_inner - HALF // 2, wide_inner) >> 3
    offset = lax.broadcasted_iota(jnp.int32, (128, LANES), 0) - (TOP + COUNT_LANE - 256)
    live = wide_lane < COUNT_LANE
    plus = (live & (offset == wide_c)).astype(F32)
    minus = (live & (offset == -wide_c) & (wide_c > 0)).astype(F32)
    counts = total[:, 256:384].astype(BF16)
    both = nn(counts, (plus + minus).astype(BF16)) * (1.0 / copies)
    differ = nn(counts, (plus - minus).astype(BF16)) * (1.0 / copies)
    partner = jnp.where(lane < HALF, pltpu.roll(total, LANES - HALF, 1), pltpu.roll(total, HALF, 1))
    differ = jnp.where(second, differ, -differ)
    out = weight * (both * total + differ * partner)
    out_ref[...] = jnp.broadcast_to(out, out_ref.shape)


def apply_kernel(pos_ref, chg_ref, w_ref, energy_ref, force_ref, real_ref, imag_ref):
    charges = chg_ref[...]
    atoms = charges.shape[1]
    cx, sx = table(pos_ref[0:1, :])
    cy, sy = table(pos_ref[1:2, :])
    cz, sz = table(pos_ref[2:3, :])
    cq = z_rows(cz, charges)
    sq = z_rows(sz, charges)
    dc = [n * sq[n] for n in range(TOP + 1)]
    ds = [-n * cq[n] for n in range(TOP + 1)]
    blank = lambda n: [jnp.zeros((n, atoms), F32)]
    w = w_ref[...].reshape(TILES * ROWS, LANES)
    w_hi, w_lo = split(w)
    first, last = slice(0, 256), slice(128, 384)
    both = lambda one, two: split(jnp.concatenate([jnp.concatenate(one, axis=0), jnp.concatenate(two, axis=0)], axis=1))
    real_ref[...] = product(
        nn, (w_hi[:, first], w_lo[:, first]), both(cq + sq + blank(80), dc + ds + blank(80))
    )
    imag_ref[...] = product(
        nn,
        (w_hi[:, last], w_lo[:, last]),
        both(blank(48) + sq + cq + blank(32), blank(48) + ds + dc + blank(32)),
    )
    zero = jnp.zeros((8, atoms), F32)
    energy, along_z, ordinary, along_y = zero, zero, zero, zero
    side_x, up_y, rest_y = zero, zero, zero
    for tile in range(30):
        re, im = pair_tile(tile, cx, sx, cy, sy)
        rows = slice(8 * tile, 8 * tile + 8)
        g, h = real_ref[rows, 0:atoms], imag_ref[rows, 0:atoms]
        energy = energy + (re * g + im * h)
        along_z = along_z + (re * real_ref[rows, atoms : 2 * atoms] + im * imag_ref[rows, atoms : 2 * atoms])
        d = im * g - re * h
        if tile < 21:
            ordinary = ordinary + d
            along_y = along_y + (tile - TOP) * d
        else:
            i, j = divmod(tile - 21, 3)
            side_x = side_x + (0.0, 9.0, 10.0)[i] * d
            if j == 0:
                up_y = up_y + d
            elif j == 1:
                up_y = up_y - d
            else:
                rest_y = rest_y + d
    n = orders((16, atoms))
    along_x = ordinary * n[0:8] + side_x
    along_y = along_y + up_y * n[0:8] + rest_y * n[8:16]
    down = lambda v: jnp.sum(v, axis=0, keepdims=True)
    energy_ref[...] = 0.25 * down(energy)
    force_ref[0:1, :] = 0.1 * down(along_x)
    force_ref[1:2, :] = 0.1 * down(along_y)
    force_ref[2:3, :] = 0.1 * down(along_z)


def call(kernel, out_shape, scratch=(), scalar=False, operands=2):
    vmem = pl.BlockSpec(memory_space=pltpu.VMEM)
    in_specs = [vmem] * operands
    if scalar:
        in_specs = [pl.BlockSpec(memory_space=pltpu.SMEM)] + in_specs
    return pl.pallas_call(
        kernel,
        out_shape=out_shape,
        in_specs=in_specs,
        out_specs=jax.tree.map(lambda _: vmem, out_shape),
        scratch_shapes=list(scratch),
        compiler_params=pltpu.CompilerParams(vmem_limit_bytes=32 * 1024 * 1024),
    )


def per_device(scale, positions, charges, miller):
    atoms = positions.shape[1]
    column = lax.axis_size(COLUMN)
    shape = lambda *s: jax.ShapeDtypeStruct(s, F32)
    tile = lax.axis_index(SPREAD).astype(jnp.int32).reshape(1)
    pairs = (TILES * ROWS, atoms)
    part = call(struct_kernel, shape(TILES, ROWS, LANES), [pltpu.VMEM(pairs, BF16)] * 4)(positions, charges)
    part = lax.all_to_all(part, SPREAD, 0, 0, tiled=True)
    part = call(collect_kernel, shape(column, ROWS, LANES), scalar=True)(tile, part, miller)
    part = lax.all_to_all(part, COLUMN, 0, 0, tiled=True)
    copies = lax.axis_size("zh")
    weigh = functools.partial(weigh_kernel, scale, copies)
    w = call(weigh, shape(TILES, ROWS, LANES), scalar=True, operands=1)(tile, part)
    w = lax.all_to_all(w, SPREAD, 0, 0, tiled=True)
    wide = (TILES * ROWS, 2 * atoms)
    energy, force = call(
        apply_kernel, (shape(1, atoms), shape(3, atoms)), [pltpu.VMEM(wide, F32)] * 2, operands=3
    )(positions, charges, w)
    return energy.reshape(atoms), force


def solution(mesh):
    fine = Mesh(mesh.devices.reshape(8, 4, 2, 4, 2), ("zl", "y", "zh", "x", "c"))
    every = fine.axis_names
    in_specs = (P(None, every), P(None, every), P(None, "zl"))
    out_specs = (P(every), P(None, every))

    def run(positions, charges, miller):
        scale = 1.0 / float(positions.shape[1]) ** 0.5
        body = functools.partial(per_device, scale)
        return jax.shard_map(body, mesh=fine, in_specs=in_specs, out_specs=out_specs, check_vma=False)(
            positions, charges, miller
        )

    return run
```

```python
import functools

import jax
import jax.numpy as jnp
import numpy as np
from jax import lax
from jax.experimental import pallas as pl
from jax.experimental.pallas import tpu as pltpu
from jax.sharding import Mesh
from jax.sharding import PartitionSpec as P

TOP = 10
TILES = 16
ROWS = 8
USED = 7
HALF = 176
LANES = 384
COUNT_LANE = 352
SIN = (3.141592640130706, -5.167710083507839, 2.550077523214083, -0.5982912856178239, 0.07765766030006041)
COS = (
    1.0,
    -4.934802137078852,
    4.058709159556494,
    -1.3352120030499017,
    0.23493731380758293,
    -0.02439632432974524,
)
F32 = jnp.float32
BF16 = jnp.bfloat16
SHAPE = (8, 4, 2, 4, 2)
AXES = ("zl", "y", "zh", "x", "c")


def column_groups():
    ids = np.arange(512).reshape(SHAPE)
    order = [(8 + n // 2 + 8 * (n % 2)) % 16 for n in range(16)]
    return [[int(ids[z % 8, y, z // 8, x, c]) for z in order] for y in range(4) for x in range(4) for c in range(2)]


def horner(coefs, u):
    out = jnp.full_like(u, coefs[-1])
    for c in coefs[-2::-1]:
        out = out * u + c
    return out


def cos_sin(turns):
    t = turns - jnp.round(turns)
    u = t * t
    s = t * horner(SIN, u)
    return 1.0 - 2.0 * s * s, 2.0 * s * horner(COS, u)


def table(coordinate):
    r = lax.broadcasted_iota(jnp.int32, (16, coordinate.shape[1]), 0)
    return cos_sin(jnp.where(r < TOP, r + 1, 0).astype(F32) * coordinate)


def late_orders(core, lanes):
    q = lax.broadcasted_iota(jnp.int32, (24, lanes), 0)
    n = jnp.where(q < 7, q, jnp.where((q >= 8) & (q < 12), q - 1, 0))
    late_a = jnp.where((q >= 12) & (q < 15), 8, jnp.where((q >= 16) & (q < 19), 9, jnp.where((q >= 19) & (q < 22), 10, 0)))
    late_b = jnp.where(late_a == 8, q - 4, jnp.where(late_a == 9, q - 8, jnp.where(late_a == 10, q - 11, 0)))
    return jnp.where(core == 0, n + late_a, late_a).astype(F32), jnp.where(core == 0, late_b, n + late_b).astype(F32)


def split(x):
    high = x.astype(BF16)
    return high, (x - high.astype(F32)).astype(BF16)


def factors(tile, cx, sx, cy, sy):
    if tile < 10:
        ca, sa, cb, sb = cx[0:8], sx[0:8], cy[tile : tile + 1], sy[tile : tile + 1]
    else:
        r = tile - 3
        ca, sa, cb, sb = cx[r : r + 1], sx[r : r + 1], cy[0:8], sy[0:8]
    return ca * cb, sa * sb, sa * cb, ca * sb


def z_rows(rows, first, charges):
    return [first] + [rows[n : n + 1] * charges for n in range(TOP)]


def nt(a, b):
    return lax.dot_general(a, b, (((1,), (1,)), ((), ())), preferred_element_type=F32)


def nn(a, b):
    return jnp.dot(a, b, preferred_element_type=F32)


def product(mul, a, b):
    return mul(a[0], b[0]) + (mul(a[0], b[1]) + mul(a[1], b[0]))


def stack(*parts):
    return jnp.concatenate([p for part in parts for p in part], axis=0)


def struct_kernel(core_ref, atoms_ref, out_ref, re_hi, re_lo, im_hi, im_lo):
    core = core_ref[0]
    both = jnp.concatenate([atoms_ref[0], atoms_ref[1]], axis=1)
    lanes = both.shape[1]
    x, z, charges = both[0:1], both[2:3], both[3:11]
    y = both[1:2] * jnp.where(core == 0, 1.0, -1.0)
    cx, sx = table(x)
    cy, sy = table(y)
    cz, sz = table(z)
    a, b = late_orders(core, lanes)
    late_c, late_s = cos_sin(a * x + b * y)
    for two in range(TILES // 2):
        real, imag = [], []
        for tile in (2 * two, 2 * two + 1):
            if tile < 13:
                cc, ss, sc, cs = factors(tile, cx, sx, cy, sy)
                real.append(cc - ss)
                imag.append(sc + cs)
            else:
                rows = slice(8 * (tile - 13), 8 * (tile - 12))
                real.append(late_c[rows])
                imag.append(late_s[rows])
        rows = slice(16 * two, 16 * two + 16)
        re_hi[rows, :], re_lo[rows, :] = split(stack(real))
        im_hi[rows, :], im_lo[rows, :] = split(stack(imag))
    cq = z_rows(cz, charges, charges)
    sq = z_rows(sz, jnp.zeros_like(charges), charges)
    blank = lambda n: [jnp.zeros((n, lanes), F32)]
    real = product(nt, (re_hi[...], re_lo[...]), split(stack(cq, sq, blank(80))))
    imag = product(nt, (im_hi[...], im_lo[...]), split(stack(blank(48), sq, cq, blank(32))))
    out_ref[:, :, 0:128] = real[:, 0:128].reshape(TILES, ROWS, 128)
    out_ref[:, :, 128:256] = (real[:, 128:256] + imag[:, 0:128]).reshape(TILES, ROWS, 128)
    out_ref[:, :, 256:384] = imag[:, 128:256].reshape(TILES, ROWS, 128)


def place_of(a, b):
    core = jnp.where(b < 0, 1, 0)
    b = jnp.abs(b)
    n = a + b
    axis = jnp.where(n <= 6, 13 * 8 + n, 14 * 8 + n - 7)
    corner = jnp.where(a == 8, 14 * 8 + b - 4, 15 * 8 + (a - 9) * 3 + b - 8)
    rest = jnp.where(a <= 7, (b - 1) * 8 + a - 1, jnp.where(b <= 7, (a + 2) * 8 + b - 1, corner))
    return core * (TILES * ROWS) + jnp.where((a == 0) | (b == 0), axis, rest)


def collect_kernel(place_ref, part_ref, miller_ref, out_ref):
    total = jnp.sum(part_ref[...], axis=0)
    a, b, c = miller_ref[0:1, :], miller_ref[1:2, :], miller_ref[2:3, :]
    sign = jnp.where((a < 0) | ((a == 0) & (b > 0)), -1, 1)
    a, b, c = a * sign, b * sign, c * sign
    listed = a.shape[1]
    row = place_of(a, b) - place_ref[0]
    pair = (row == lax.broadcasted_iota(jnp.int32, (ROWS, listed), 0)).astype(F32)
    lane = c + (TOP + COUNT_LANE - 256)
    third = (lane == lax.broadcasted_iota(jnp.int32, (128, listed), 0)).astype(F32)
    counts = nt(pair.astype(BF16), third.astype(BF16))
    copies = out_ref.shape[0]
    for r in range(USED):
        out_ref[:, :, LANES * r : LANES * r + 256] = jnp.broadcast_to(total[r : r + 1, 0:256], (copies, 1, 256))
        last = total[r : r + 1, 256:384] + counts[r : r + 1]
        out_ref[:, :, LANES * r + 256 : LANES * r + 384] = jnp.broadcast_to(last, (copies, 1, 128))


def weigh_kernel(scale, copies, tile_ref, part_ref, out_ref):
    flat = jnp.sum(part_ref[...], axis=0)
    total = stack([flat[:, LANES * r : LANES * r + LANES] for r in range(USED)], [jnp.zeros((1, LANES), F32)])
    tile = tile_ref[0]
    row = lax.broadcasted_iota(jnp.int32, (ROWS, LANES), 0)
    lane = lax.broadcasted_iota(jnp.int32, (ROWS, LANES), 1)
    inner = jnp.where(lane >= HALF, lane - HALF, lane)
    second = inner >= HALF // 2
    c = jnp.where(second, inner - HALF // 2, inner) >> 3
    a = jnp.where(tile < 10, tile + 1, jnp.where(tile < 13, tile - 2, 0))
    b = row + 1
    a = jnp.where(tile == 13, 0, jnp.where(tile == 14, jnp.where(row < 4, 0, 8), a))
    b = jnp.where(tile == 13, row, jnp.where(tile == 14, jnp.where(row < 4, row + 7, row + 4), b))
    a = jnp.where(tile == 15, jnp.where(row < 3, 9, 10), a)
    b = jnp.where(tile == 15, jnp.where(row < 3, row + 8, row + 5), b)
    square = jnp.maximum(a * a + b * b + c * c, 1).astype(F32)
    weight = jnp.exp(-0.025 * square) / square * scale
    wide_lane = lax.broadcasted_iota(jnp.int32, (128, LANES), 1)
    wide_inner = jnp.where(wide_lane >= HALF, wide_lane - HALF, wide_lane)
    wide_c = jnp.where(wide_inner >= HALF // 2, wide_inner - HALF // 2, wide_inner) >> 3
    offset = lax.broadcasted_iota(jnp.int32, (128, LANES), 0) - (TOP + COUNT_LANE - 256)
    live = wide_lane < COUNT_LANE
    plus = (live & (offset == wide_c)).astype(F32)
    minus = (live & (offset == -wide_c) & (wide_c > 0)).astype(F32)
    counts = total[:, 256:384].astype(BF16)
    both = nn(counts, (plus + minus).astype(BF16)) * (1.0 / copies)
    differ = nn(counts, (plus - minus).astype(BF16)) * (1.0 / copies)
    partner = jnp.where(lane < HALF, pltpu.roll(total, LANES - HALF, 1), pltpu.roll(total, HALF, 1))
    differ = jnp.where(second, differ, -differ)
    out = weight * (both * total + differ * partner)
    out_ref[...] = jnp.broadcast_to(out, out_ref.shape)


def apply_kernel(atoms_ref, w_ref, energy_ref, force_ref, real_ref, imag_ref):
    x, y, z, charges = atoms_ref[0:1, :], atoms_ref[1:2, :], atoms_ref[2:3, :], atoms_ref[3:11, :]
    atoms = x.shape[1]
    cx, sx = table(x)
    cy, sy = table(y)
    cz, sz = table(z)
    none = jnp.zeros_like(charges)
    cq = z_rows(cz, charges, charges)
    sq = z_rows(sz, none, charges)
    dc = [n * sq[n] for n in range(TOP + 1)]
    ds = [-n * cq[n] for n in range(TOP + 1)]
    blank = lambda n: [jnp.zeros((n, atoms), F32)]
    w_hi, w_lo = split(w_ref[...].reshape(2 * TILES * ROWS, LANES))
    first, last = slice(0, 256), slice(128, 384)
    beside = lambda one, two: split(jnp.concatenate([stack(*one), stack(*two)], axis=1))
    real_ref[...] = product(
        nn, (w_hi[:, first], w_lo[:, first]), beside((cq, sq, blank(80)), (dc, ds, blank(80)))
    )
    imag_ref[...] = product(
        nn,
        (w_hi[:, last], w_lo[:, last]),
        beside((blank(48), sq, cq, blank(32)), (blank(48), ds, dc, blank(32))),
    )
    zero = jnp.zeros((8, atoms), F32)
    sums = {"e": zero, "z": zero, "x": zero, "y": zero, "x_row": zero, "y_row": zero}

    def add(core, tile, re, im):
        rows = slice(8 * (core * TILES + tile), 8 * (core * TILES + tile) + 8)
        g, h = real_ref[rows, 0:atoms], imag_ref[rows, 0:atoms]
        sums["e"] += re * g + im * h
        sums["z"] += re * real_ref[rows, atoms : 2 * atoms] + im * imag_ref[rows, atoms : 2 * atoms]
        return im * g - re * h

    for tile in range(13):
        cc, ss, sc, cs = factors(tile, cx, sx, cy, sy)
        up, down = add(0, tile, cc - ss, sc + cs), add(1, tile, cc + ss, sc - cs)
        if tile < 10:
            sums["x_row"] += up + down
            sums["y"] += (tile + 1.0) * (up - down)
        else:
            sums["x"] += (tile - 2.0) * (up + down)
            sums["y_row"] += up - down
    for core in range(2):
        a, b = late_orders(core, atoms)
        b = b * (1.0 - 2.0 * core)
        late_c, late_s = cos_sin(a * x + b * y)
        for j in range(3):
            rows = slice(8 * j, 8 * j + 8)
            d = add(core, 13 + j, late_c[rows], late_s[rows])
            sums["x"] += a[rows] * d
            sums["y"] += b[rows] * d
    order = lax.broadcasted_iota(jnp.int32, (8, atoms), 0).astype(F32) + 1.0
    down = lambda v: jnp.sum(v, axis=0, keepdims=True)
    energy_ref[...] = 0.25 * down(sums["e"])
    force_ref[0:1, :] = 0.1 * down(sums["x"] + order * sums["x_row"])
    force_ref[1:2, :] = 0.1 * down(sums["y"] + order * sums["y_row"])
    force_ref[2:3, :] = 0.1 * down(sums["z"])


def call(kernel, out_shape, operands, scratch=(), scalar=False):
    vmem = pl.BlockSpec(memory_space=pltpu.VMEM)
    in_specs = [vmem] * operands
    if scalar:
        in_specs = [pl.BlockSpec(memory_space=pltpu.SMEM)] + in_specs
    return pl.pallas_call(
        kernel,
        out_shape=out_shape,
        in_specs=in_specs,
        out_specs=jax.tree.map(lambda _: vmem, out_shape),
        scratch_shapes=list(scratch),
        compiler_params=pltpu.CompilerParams(vmem_limit_bytes=32 * 1024 * 1024),
    )


def per_device(scale, positions, charges, miller):
    atoms = positions.shape[1]
    column = lax.axis_size("zl") * lax.axis_size("zh")
    copies = lax.axis_size("zh")
    shape = lambda *s: jax.ShapeDtypeStruct(s, F32)
    core = lax.axis_index("c").astype(jnp.int32).reshape(1)
    tile = lax.axis_index(("y", "x")).astype(jnp.int32).reshape(1)
    place = core * (TILES * ROWS) + tile * ROWS
    own = jnp.concatenate([positions, charges], axis=0)
    pair = lax.all_gather(own, "c")
    half = [pltpu.VMEM((TILES * ROWS, 2 * atoms), BF16)] * 4
    part = call(struct_kernel, shape(TILES, ROWS, LANES), 1, half, scalar=True)(core, pair)
    part = lax.all_to_all(part, ("y", "x"), 0, 0, tiled=True)
    part = call(collect_kernel, shape(column, 1, USED * LANES), 2, scalar=True)(place, part, miller)
    part = lax.all_to_all(part, AXES, 0, 0, axis_index_groups=column_groups(), tiled=True)
    weigh = functools.partial(weigh_kernel, scale, copies)
    w = call(weigh, shape(TILES, ROWS, LANES), 1, scalar=True)(tile, part)
    w = lax.all_to_all(w, ("y", "x"), 0, 0, tiled=True)
    w = lax.all_gather(w, "c")
    wide = [pltpu.VMEM((2 * TILES * ROWS, 2 * atoms), F32)] * 2
    energy, force = call(apply_kernel, (shape(1, atoms), shape(3, atoms)), 2, wide)(own, w)
    return energy.reshape(atoms), force


def solution(mesh):
    fine = Mesh(mesh.devices.reshape(SHAPE), AXES)
    in_specs = (P(None, AXES), P(None, AXES), P(None, "zl"))
    out_specs = (P(AXES), P(None, AXES))

    def run(positions, charges, miller):
        scale = 1.0 / float(positions.shape[1]) ** 0.5
        body = functools.partial(per_device, scale)
        return jax.shard_map(body, mesh=fine, in_specs=in_specs, out_specs=out_specs, check_vma=False)(
            positions, charges, miller
        )

    return run
```

```python
import functools

import jax
import jax.numpy as jnp
import numpy as np
from jax import lax
from jax.experimental import pallas as pl
from jax.experimental.pallas import tpu as pltpu
from jax.sharding import Mesh
from jax.sharding import PartitionSpec as P

TOP = 10
TILES = 16
ROWS = 8
USED = 7
HALF = 176
LANES = 384
COUNT_LANE = 352
SIN = (3.141592640130706, -5.167710083507839, 2.550077523214083, -0.5982912856178239, 0.07765766030006041)
COS = (
    1.0,
    -4.934802137078852,
    4.058709159556494,
    -1.3352120030499017,
    0.23493731380758293,
    -0.02439632432974524,
)
F32 = jnp.float32
BF16 = jnp.bfloat16
SHAPE = (8, 4, 2, 4, 2)
AXES = ("zl", "y", "zh", "x", "c")
ROOT = (2, 2)


def column_groups():
    ids = np.arange(512).reshape(SHAPE)
    order = [(8 + n // 2 + 8 * (n % 2)) % 16 for n in range(16)]
    return [[int(ids[z % 8, y, z // 8, x, c]) for z in order] for y in range(4) for x in range(4) for c in range(2)]


def plane_groups():
    ids = np.arange(512).reshape(SHAPE)
    order = [((n // 4 + ROOT[0]) % 4, (n % 4 + ROOT[1]) % 4) for n in range(16)]
    rest = [(zl, zh, c) for zl in range(8) for zh in range(2) for c in range(2)]
    return [[int(ids[zl, y, zh, x, c]) for y, x in order] for zl, zh, c in rest]


def horner(coefs, u):
    out = jnp.full_like(u, coefs[-1])
    for c in coefs[-2::-1]:
        out = out * u + c
    return out


def cos_sin(turns):
    t = turns - jnp.round(turns)
    u = t * t
    s = t * horner(SIN, u)
    return 1.0 - 2.0 * s * s, 2.0 * s * horner(COS, u)


def table(coordinate):
    r = lax.broadcasted_iota(jnp.int32, (16, coordinate.shape[1]), 0)
    return cos_sin(jnp.where(r < TOP, r + 1, 0).astype(F32) * coordinate)


def late_orders(core, lanes):
    q = lax.broadcasted_iota(jnp.int32, (24, lanes), 0)
    n = jnp.where(q < 7, q, jnp.where((q >= 8) & (q < 12), q - 1, 0))
    late_a = jnp.where((q >= 12) & (q < 15), 8, jnp.where((q >= 16) & (q < 19), 9, jnp.where((q >= 19) & (q < 22), 10, 0)))
    late_b = jnp.where(late_a == 8, q - 4, jnp.where(late_a == 9, q - 8, jnp.where(late_a == 10, q - 11, 0)))
    return jnp.where(core == 0, n + late_a, late_a).astype(F32), jnp.where(core == 0, late_b, n + late_b).astype(F32)


def split(x):
    high = x.astype(BF16)
    return high, (x - high.astype(F32)).astype(BF16)


def factors(tile, cx, sx, cy, sy):
    if tile < 10:
        ca, sa, cb, sb = cx[0:8], sx[0:8], cy[tile : tile + 1], sy[tile : tile + 1]
    else:
        r = tile - 3
        ca, sa, cb, sb = cx[r : r + 1], sx[r : r + 1], cy[0:8], sy[0:8]
    return ca * cb, sa * sb, sa * cb, ca * sb


def z_rows(rows, first, charges):
    return [first] + [rows[n : n + 1] * charges for n in range(TOP)]


def nt(a, b):
    return lax.dot_general(a, b, (((1,), (1,)), ((), ())), preferred_element_type=F32)


def nn(a, b):
    return jnp.dot(a, b, preferred_element_type=F32)


def stack(*parts):
    return jnp.concatenate([p for part in parts for p in part], axis=0)


def struct_kernel(place_ref, atoms_ref, out_ref, counts_ref, pairs_ref):
    place = place_ref[0]
    core = jnp.where(place < TILES * ROWS, 0, 1)
    listed = [atoms_ref[0, r : r + 1, :].astype(jnp.int32) for r in (11, 12, 13)]
    counts_ref[...] = count_listed(place, *listed)
    both = jnp.concatenate([atoms_ref[0], atoms_ref[1]], axis=1)
    lanes = both.shape[1]
    x, z, charges = both[8:9], both[10:11], both[0:8]
    y = both[9:10] * jnp.where(core == 0, 1.0, -1.0)
    cx, sx = table(x)
    cy, sy = table(y)
    cz, sz = table(z)
    a, b = late_orders(core, lanes)
    late_c, late_s = cos_sin(a * x + b * y)

    def keep(rows, value):
        high, low = split(value)
        pairs_ref[rows, 0:lanes] = high
        pairs_ref[rows, lanes : 2 * lanes] = low
        pairs_ref[rows, 2 * lanes : 3 * lanes] = high

    for two in range(TILES // 2):
        real, imag = [], []
        for tile in (2 * two, 2 * two + 1):
            if tile < 13:
                cc, ss, sc, cs = factors(tile, cx, sx, cy, sy)
                real.append(cc - ss)
                imag.append(sc + cs)
            else:
                rows = slice(8 * (tile - 13), 8 * (tile - 12))
                real.append(late_c[rows])
                imag.append(late_s[rows])
        keep(slice(16 * two, 16 * two + 16), stack(real))
        keep(slice(128 + 16 * two, 128 + 16 * two + 16), stack(imag))
    cq = z_rows(cz, charges, charges)
    sq = z_rows(sz, jnp.zeros_like(charges), charges)
    high, low = split(stack(cq, sq, [jnp.zeros((256 - HALF, lanes), F32)]))
    sums = nt(pairs_ref[...], jnp.concatenate([high, high, low], axis=1))
    real, imag = sums[0:128], pltpu.roll(sums[128:256], HALF - 128, 1)
    out_ref[:, :, 0:128] = real[:, 0:128].reshape(TILES, ROWS, 128)
    out_ref[:, :, 128:256] = (real[:, 128:256] + imag[:, 0:128]).reshape(TILES, ROWS, 128)
    out_ref[:, :, 256:384] = imag[:, 128:256].reshape(TILES, ROWS, 128)


def place_of(a, b):
    core = jnp.where(b < 0, 1, 0)
    b = jnp.abs(b)
    n = a + b
    axis = jnp.where(n <= 6, 13 * 8 + n, 14 * 8 + n - 7)
    corner = jnp.where(a == 8, 14 * 8 + b - 4, 15 * 8 + (a - 9) * 3 + b - 8)
    rest = jnp.where(a <= 7, (b - 1) * 8 + a - 1, jnp.where(b <= 7, (a + 2) * 8 + b - 1, corner))
    return core * (TILES * ROWS) + jnp.where((a == 0) | (b == 0), axis, rest)


def count_listed(place, a, b, c):
    sign = jnp.where((a < 0) | ((a == 0) & (b > 0)), -1, 1)
    a, b, c = a * sign, b * sign, c * sign
    listed = a.shape[1]
    row = place_of(a, b) - place
    pair = (row == lax.broadcasted_iota(jnp.int32, (ROWS, listed), 0)).astype(F32)
    lane = c + (TOP + COUNT_LANE - 256)
    third = (lane == lax.broadcasted_iota(jnp.int32, (128, listed), 0)).astype(F32)
    return nt(pair.astype(BF16), third.astype(BF16))


def collect_kernel(part_ref, counts_ref, out_ref):
    total = jnp.sum(part_ref[...], axis=0)
    copies = out_ref.shape[0]
    for r in range(USED):
        out_ref[:, :, LANES * r : LANES * r + 256] = jnp.broadcast_to(total[r : r + 1, 0:256], (copies, 1, 256))
        last = total[r : r + 1, 256:384] + counts_ref[r : r + 1, :]
        out_ref[:, :, LANES * r + 256 : LANES * r + 384] = jnp.broadcast_to(last, (copies, 1, 128))


def weigh_kernel(scale, copies, tile_ref, part_ref, out_ref):
    flat = jnp.sum(part_ref[...], axis=0)
    total = stack([flat[:, LANES * r : LANES * r + LANES] for r in range(USED)], [jnp.zeros((1, LANES), F32)])
    tile = tile_ref[0]
    row = lax.broadcasted_iota(jnp.int32, (ROWS, LANES), 0)
    lane = lax.broadcasted_iota(jnp.int32, (ROWS, LANES), 1)
    inner = jnp.where(lane >= HALF, lane - HALF, lane)
    second = inner >= HALF // 2
    c = jnp.where(second, inner - HALF // 2, inner) >> 3
    a = jnp.where(tile < 10, tile + 1, jnp.where(tile < 13, tile - 2, 0))
    b = row + 1
    a = jnp.where(tile == 13, 0, jnp.where(tile == 14, jnp.where(row < 4, 0, 8), a))
    b = jnp.where(tile == 13, row, jnp.where(tile == 14, jnp.where(row < 4, row + 7, row + 4), b))
    a = jnp.where(tile == 15, jnp.where(row < 3, 9, 10), a)
    b = jnp.where(tile == 15, jnp.where(row < 3, row + 8, row + 5), b)
    square = jnp.maximum(a * a + b * b + c * c, 1).astype(F32)
    weight = jnp.exp(-0.025 * square) / square * scale
    wide_lane = lax.broadcasted_iota(jnp.int32, (128, LANES), 1)
    wide_inner = jnp.where(wide_lane >= HALF, wide_lane - HALF, wide_lane)
    wide_c = jnp.where(wide_inner >= HALF // 2, wide_inner - HALF // 2, wide_inner) >> 3
    offset = lax.broadcasted_iota(jnp.int32, (128, LANES), 0) - (TOP + COUNT_LANE - 256)
    live = wide_lane < COUNT_LANE
    plus = (live & (offset == wide_c)).astype(F32)
    minus = (live & (offset == -wide_c) & (wide_c > 0)).astype(F32)
    counts = total[:, 256:384].astype(BF16)
    both = nn(counts, (plus + minus).astype(BF16)) * (1.0 / copies)
    differ = nn(counts, (plus - minus).astype(BF16)) * (1.0 / copies)
    near, far = HALF // 2, HALF + HALF // 2
    ahead = jnp.where(second, pltpu.roll(total, LANES - near, 1), pltpu.roll(total, LANES - far, 1))
    behind = jnp.where(second, pltpu.roll(total, far, 1), pltpu.roll(total, near, 1))
    partner = jnp.where(lane < HALF, ahead, behind)
    differ = jnp.where(second == (lane < HALF), differ, -differ)
    out = weight * (both * total + differ * partner)
    out_ref[...] = jnp.broadcast_to(out, out_ref.shape)


def apply_kernel(atoms_ref, w_ref, energy_ref, force_ref, turned_ref):
    x, y, z, charges = atoms_ref[8:9, :], atoms_ref[9:10, :], atoms_ref[10:11, :], atoms_ref[0:8, :]
    atoms = x.shape[1]
    cx, sx = table(x)
    cy, sy = table(y)
    cz, sz = table(z)
    none = jnp.zeros_like(charges)
    cq = z_rows(cz, charges, charges)
    sq = z_rows(sz, none, charges)
    dc = [n * sq[n] for n in range(TOP + 1)]
    ds = [-n * cq[n] for n in range(TOP + 1)]
    blank = [jnp.zeros((256 - HALF, atoms), F32)]
    high, low = split(jnp.concatenate([stack(cq, sq, blank), stack(dc, ds, blank)], axis=1))
    w = w_ref[...].reshape(2 * TILES * ROWS, LANES)
    w = jnp.concatenate([w[:, 0:256], pltpu.roll(w[:, 128:384], 256 - (HALF - 128), 1)], axis=0)
    w_high, w_low = split(w)
    turned_ref[...] = nn(jnp.concatenate([w_high, w_low, w_high], axis=1), jnp.concatenate([high, high, low], axis=0))
    zero = jnp.zeros((8, atoms), F32)
    sums = {"e": zero, "z": zero, "x": zero, "y": zero, "x_row": zero, "y_row": zero}

    def add(core, tile, re, im):
        at = 8 * (core * TILES + tile)
        real, imag = slice(at, at + 8), slice(at + 2 * TILES * ROWS, at + 2 * TILES * ROWS + 8)
        g, h = turned_ref[real, 0:atoms], turned_ref[imag, 0:atoms]
        sums["e"] += re * g + im * h
        sums["z"] += re * turned_ref[real, atoms : 2 * atoms] + im * turned_ref[imag, atoms : 2 * atoms]
        return im * g - re * h

    for tile in range(13):
        cc, ss, sc, cs = factors(tile, cx, sx, cy, sy)
        up, down = add(0, tile, cc - ss, sc + cs), add(1, tile, cc + ss, sc - cs)
        if tile < 10:
            sums["x_row"] += up + down
            sums["y"] += (tile + 1.0) * (up - down)
        else:
            sums["x"] += (tile - 2.0) * (up + down)
            sums["y_row"] += up - down
    for core in range(2):
        a, b = late_orders(core, atoms)
        b = b * (1.0 - 2.0 * core)
        late_c, late_s = cos_sin(a * x + b * y)
        for j in range(3):
            rows = slice(8 * j, 8 * j + 8)
            d = add(core, 13 + j, late_c[rows], late_s[rows])
            sums["x"] += a[rows] * d
            sums["y"] += b[rows] * d
    order = lax.broadcasted_iota(jnp.int32, (8, atoms), 0).astype(F32) + 1.0
    down = lambda v: jnp.sum(v, axis=0, keepdims=True)
    energy_ref[...] = 0.25 * down(sums["e"])
    force_ref[0:1, :] = 0.1 * down(sums["x"] + order * sums["x_row"])
    force_ref[1:2, :] = 0.1 * down(sums["y"] + order * sums["y_row"])
    force_ref[2:3, :] = 0.1 * down(sums["z"])


def call(kernel, out_shape, operands, scratch=(), scalar=False):
    vmem = pl.BlockSpec(memory_space=pltpu.VMEM)
    in_specs = [vmem] * operands
    if scalar:
        in_specs = [pl.BlockSpec(memory_space=pltpu.SMEM)] + in_specs
    return pl.pallas_call(
        kernel,
        out_shape=out_shape,
        in_specs=in_specs,
        out_specs=jax.tree.map(lambda _: vmem, out_shape),
        scratch_shapes=list(scratch),
        compiler_params=pltpu.CompilerParams(vmem_limit_bytes=32 * 1024 * 1024),
    )


def per_device(scale, positions, charges, miller):
    atoms = positions.shape[1]
    column = lax.axis_size("zl") * lax.axis_size("zh")
    copies = lax.axis_size("zh")
    shape = lambda *s: jax.ShapeDtypeStruct(s, F32)
    core = lax.axis_index("c").astype(jnp.int32).reshape(1)
    from_root = [(lax.axis_index(axis).astype(jnp.int32) + (4 - at)) % 4 for axis, at in zip(("y", "x"), ROOT)]
    tile = (from_root[0] * 4 + from_root[1]).reshape(1)
    place = core * (TILES * ROWS) + tile * ROWS
    own = jnp.concatenate([charges, positions, miller.astype(F32)], axis=0)
    pair = lax.all_gather(own, "c")
    half = [pltpu.VMEM((2 * TILES * ROWS, 6 * atoms), BF16)]
    sums = (shape(TILES, ROWS, LANES), shape(ROWS, 128))
    part, counts = call(struct_kernel, sums, 1, half, scalar=True)(place, pair)
    part = lax.all_to_all(part, AXES, 0, 0, axis_index_groups=plane_groups(), tiled=True)
    part = call(collect_kernel, shape(column, 1, USED * LANES), 2)(part, counts)
    part = lax.all_to_all(part, AXES, 0, 0, axis_index_groups=column_groups(), tiled=True)
    weigh = functools.partial(weigh_kernel, scale, copies)
    w = call(weigh, shape(TILES, ROWS, LANES), 1, scalar=True)(tile, part)
    w = lax.all_to_all(w, AXES, 0, 0, axis_index_groups=plane_groups(), tiled=True)
    w = lax.all_gather(w, "c")
    wide = [pltpu.VMEM((4 * TILES * ROWS, 2 * atoms), F32)]
    energy, force = call(apply_kernel, (shape(1, atoms), shape(3, atoms)), 2, wide)(own, w)
    return energy.reshape(atoms), force


def solution(mesh):
    fine = Mesh(mesh.devices.reshape(SHAPE), AXES)
    in_specs = (P(None, AXES), P(None, AXES), P(None, "zl"))
    out_specs = (P(AXES), P(None, AXES))

    def run(positions, charges, miller):
        scale = 1.0 / float(positions.shape[1]) ** 0.5
        body = functools.partial(per_device, scale)
        return jax.shard_map(body, mesh=fine, in_specs=in_specs, out_specs=out_specs, check_vma=False)(
            positions, charges, miller
        )

    return run
```

```python
import functools

import jax
import jax.numpy as jnp
import numpy as np
from jax import lax
from jax.experimental import pallas as pl
from jax.experimental.pallas import tpu as pltpu
from jax.sharding import Mesh
from jax.sharding import PartitionSpec as P

TOP = 10
TILES = 16
ROWS = 8
HALVES = 2 * TILES
SHARD = 4
HALF = 176
LANES = 384
COUNT_LANE = 352
SIN = (3.141592640130706, -5.167710083507839, 2.550077523214083, -0.5982912856178239, 0.07765766030006041)
COS = (
    1.0,
    -4.934802137078852,
    4.058709159556494,
    -1.3352120030499017,
    0.23493731380758293,
    -0.02439632432974524,
)
F32 = jnp.float32
BF16 = jnp.bfloat16
SHAPE = (8, 4, 2, 4, 2)
AXES = ("zl", "y", "zh", "x", "c")
ROOT = (2, 2)


def device(z, y, x, c):
    return int(np.arange(512).reshape(SHAPE)[z % 8, y, z // 8, x, c])


def layer_groups():
    chips = [((n // 4 + ROOT[0]) % 4, (n % 4 + ROOT[1]) % 4) for n in range(TILES)]
    return [[device(z + half, y, x, c) for y, x in chips for half in (0, 1)] for z in range(0, 16, 2) for c in (0, 1)]


def column_groups():
    order = [(8 + n // 2 * 2 + 8 * (n % 2)) % 16 for n in range(8)]
    rest = [(half, y, x, c) for half in (0, 1) for y in range(4) for x in range(4) for c in (0, 1)]
    return [[device(z + half, y, x, c) for z in order] for half, y, x, c in rest]


def horner(coefs, u):
    out = jnp.full_like(u, coefs[-1])
    for c in coefs[-2::-1]:
        out = out * u + c
    return out


def cos_sin(turns):
    t = turns - jnp.round(turns)
    u = t * t
    s = t * horner(SIN, u)
    return 1.0 - 2.0 * s * s, 2.0 * s * horner(COS, u)


def table(coordinate):
    r = lax.broadcasted_iota(jnp.int32, (16, coordinate.shape[1]), 0)
    return cos_sin(jnp.where(r < TOP, r + 1, 0).astype(F32) * coordinate)


def late_orders(core, lanes):
    q = lax.broadcasted_iota(jnp.int32, (24, lanes), 0)
    n = jnp.where(q < 7, q, jnp.where((q >= 8) & (q < 12), q - 1, 0))
    late_a = jnp.where((q >= 12) & (q < 15), 8, jnp.where((q >= 16) & (q < 19), 9, jnp.where((q >= 19) & (q < 22), 10, 0)))
    late_b = jnp.where(late_a == 8, q - 4, jnp.where(late_a == 9, q - 8, jnp.where(late_a == 10, q - 11, 0)))
    return jnp.where(core == 0, n + late_a, late_a).astype(F32), jnp.where(core == 0, late_b, n + late_b).astype(F32)


def split(x):
    high = x.astype(BF16)
    return high, (x - high.astype(F32)).astype(BF16)


def factors(tile, cx, sx, cy, sy):
    if tile < 10:
        ca, sa, cb, sb = cx[0:8], sx[0:8], cy[tile : tile + 1], sy[tile : tile + 1]
    else:
        r = tile - 3
        ca, sa, cb, sb = cx[r : r + 1], sx[r : r + 1], cy[0:8], sy[0:8]
    return ca * cb, sa * sb, sa * cb, ca * sb


def z_rows(rows, first, charges):
    return [first] + [rows[n : n + 1] * charges for n in range(TOP)]


def nt(a, b):
    return lax.dot_general(a, b, (((1,), (1,)), ((), ())), preferred_element_type=F32)


def nn(a, b):
    return jnp.dot(a, b, preferred_element_type=F32)


def stack(*parts):
    return jnp.concatenate([p for part in parts for p in part], axis=0)


def struct_kernel(where_ref, atoms_ref, out_ref, pairs_ref):
    core, mine = where_ref[0] // HALVES, where_ref[0] % HALVES // 2
    both = jnp.concatenate([atoms_ref[0], atoms_ref[1]], axis=1)
    lanes = both.shape[1]
    x, z, charges = both[8:9], both[10:11], both[0:8]
    y = both[9:10] * jnp.where(core == 0, 1.0, -1.0)
    cx, sx = table(x)
    cy, sy = table(y)
    cz, sz = table(z)
    a, b = late_orders(core, lanes)
    late_c, late_s = cos_sin(a * x + b * y)

    def keep(rows, value):
        high, low = split(value)
        pairs_ref[rows, 0:lanes] = high
        pairs_ref[rows, lanes : 2 * lanes] = low
        pairs_ref[rows, 2 * lanes : 3 * lanes] = high

    for two in range(TILES // 2):
        real, imag = [], []
        for tile in (2 * two, 2 * two + 1):
            if tile < 13:
                cc, ss, sc, cs = factors(tile, cx, sx, cy, sy)
                real.append(cc - ss)
                imag.append(sc + cs)
            else:
                rows = slice(8 * (tile - 13), 8 * (tile - 12))
                real.append(late_c[rows])
                imag.append(late_s[rows])
        keep(slice(16 * two, 16 * two + 16), stack(real))
        keep(slice(128 + 16 * two, 128 + 16 * two + 16), stack(imag))
    cq = z_rows(cz, charges, charges)
    sq = z_rows(sz, jnp.zeros_like(charges), charges)
    high, low = split(stack(cq, sq, [jnp.zeros((256 - HALF, lanes), F32)]))
    sums = nt(pairs_ref[...], jnp.concatenate([high, high, low], axis=1))
    real, imag = sums[0:128], pltpu.roll(sums[128:256], HALF - 128, 1)
    middle = real[:, 128:256] + imag[:, 0:128]
    for n in range(HALVES):
        rows = slice(SHARD * n, SHARD * n + SHARD)
        out_ref[n, :, 0:128] = real[rows, 0:128]
        out_ref[n, :, 128:256] = middle[rows]
        out_ref[n, :, 256:384] = imag[rows, 128:256]
    listed = [atoms_ref[0, r : r + 1, :].astype(jnp.int32) for r in (11, 12, 13)]
    counts = count_listed((core * TILES + mine) * ROWS, *listed)
    for half in range(2):
        own = out_ref.at[2 * mine + half, :, 256:384]
        own[...] = own[...] + counts[SHARD * half : SHARD * half + SHARD]


def place_of(a, b):
    core = jnp.where(b < 0, 1, 0)
    b = jnp.abs(b)
    n = a + b
    axis = jnp.where(n <= 6, 13 * 8 + n, 14 * 8 + n - 7)
    corner = jnp.where(a == 8, 14 * 8 + b - 4, 15 * 8 + (a - 9) * 3 + b - 8)
    rest = jnp.where(a <= 7, (b - 1) * 8 + a - 1, jnp.where(b <= 7, (a + 2) * 8 + b - 1, corner))
    return core * (TILES * ROWS) + jnp.where((a == 0) | (b == 0), axis, rest)


def count_listed(place, a, b, c):
    sign = jnp.where((a < 0) | ((a == 0) & (b > 0)), -1, 1)
    a, b, c = a * sign, b * sign, c * sign
    listed = a.shape[1]
    row = place_of(a, b) - place
    pair = (row == lax.broadcasted_iota(jnp.int32, (ROWS, listed), 0)).astype(F32)
    lane = c + (TOP + COUNT_LANE - 256)
    third = (lane == lax.broadcasted_iota(jnp.int32, (128, listed), 0)).astype(F32)
    return nt(pair.astype(BF16), third.astype(BF16))


def collect_kernel(part_ref, out_ref):
    out_ref[...] = jnp.broadcast_to(jnp.sum(part_ref[...], axis=0), out_ref.shape)


def weigh_kernel(scale, copies, where_ref, part_ref, out_ref):
    total = stack([jnp.sum(part_ref[...], axis=0), jnp.zeros((ROWS - SHARD, LANES), F32)])
    tile = where_ref[0] % HALVES // 2
    row = lax.broadcasted_iota(jnp.int32, (ROWS, LANES), 0) + SHARD * (where_ref[0] % 2)
    lane = lax.broadcasted_iota(jnp.int32, (ROWS, LANES), 1)
    inner = jnp.where(lane >= HALF, lane - HALF, lane)
    second = inner >= HALF // 2
    c = jnp.where(second, inner - HALF // 2, inner) >> 3
    a = jnp.where(tile < 10, tile + 1, jnp.where(tile < 13, tile - 2, 0))
    b = row + 1
    a = jnp.where(tile == 13, 0, jnp.where(tile == 14, jnp.where(row < 4, 0, 8), a))
    b = jnp.where(tile == 13, row, jnp.where(tile == 14, jnp.where(row < 4, row + 7, row + 4), b))
    a = jnp.where(tile == 15, jnp.where(row < 3, 9, 10), a)
    b = jnp.where(tile == 15, jnp.where(row < 3, row + 8, row + 5), b)
    square = jnp.maximum(a * a + b * b + c * c, 1).astype(F32)
    weight = jnp.exp(-0.025 * square) / square * scale
    wide_lane = lax.broadcasted_iota(jnp.int32, (128, LANES), 1)
    wide_inner = jnp.where(wide_lane >= HALF, wide_lane - HALF, wide_lane)
    wide_c = jnp.where(wide_inner >= HALF // 2, wide_inner - HALF // 2, wide_inner) >> 3
    offset = lax.broadcasted_iota(jnp.int32, (128, LANES), 0) - (TOP + COUNT_LANE - 256)
    live = wide_lane < COUNT_LANE
    plus = (live & (offset == wide_c)).astype(F32)
    minus = (live & (offset == -wide_c) & (wide_c > 0)).astype(F32)
    counts = total[:, 256:384].astype(BF16)
    both = nn(counts, (plus + minus).astype(BF16)) * (1.0 / copies)
    differ = nn(counts, (plus - minus).astype(BF16)) * (1.0 / copies)
    near, far = HALF // 2, HALF + HALF // 2
    ahead = jnp.where(second, pltpu.roll(total, LANES - near, 1), pltpu.roll(total, LANES - far, 1))
    behind = jnp.where(second, pltpu.roll(total, far, 1), pltpu.roll(total, near, 1))
    partner = jnp.where(lane < HALF, ahead, behind)
    differ = jnp.where(second == (lane < HALF), differ, -differ)
    out = weight * (both * total + differ * partner)
    out_ref[...] = jnp.broadcast_to(out[0:SHARD], out_ref.shape)


def apply_kernel(atoms_ref, w_ref, energy_ref, force_ref, turned_ref):
    x, y, z, charges = atoms_ref[8:9, :], atoms_ref[9:10, :], atoms_ref[10:11, :], atoms_ref[0:8, :]
    atoms = x.shape[1]
    cx, sx = table(x)
    cy, sy = table(y)
    cz, sz = table(z)
    none = jnp.zeros_like(charges)
    cq = z_rows(cz, charges, charges)
    sq = z_rows(sz, none, charges)
    dc = [n * sq[n] for n in range(TOP + 1)]
    ds = [-n * cq[n] for n in range(TOP + 1)]
    blank = [jnp.zeros((256 - HALF, atoms), F32)]
    high, low = split(jnp.concatenate([stack(cq, sq, blank), stack(dc, ds, blank)], axis=1))
    w = stack([w_ref[core, n] for core in range(2) for n in range(HALVES)])
    w = jnp.concatenate([w[:, 0:256], pltpu.roll(w[:, 128:384], 256 - (HALF - 128), 1)], axis=0)
    w_high, w_low = split(w)
    turned_ref[...] = nn(jnp.concatenate([w_high, w_low, w_high], axis=1), jnp.concatenate([high, high, low], axis=0))
    zero = jnp.zeros((8, atoms), F32)
    sums = {"e": zero, "z": zero, "x": zero, "y": zero, "x_row": zero, "y_row": zero}

    def add(core, tile, re, im):
        at = 8 * (core * TILES + tile)
        real, imag = slice(at, at + 8), slice(at + 2 * TILES * ROWS, at + 2 * TILES * ROWS + 8)
        g, h = turned_ref[real, 0:atoms], turned_ref[imag, 0:atoms]
        sums["e"] += re * g + im * h
        sums["z"] += re * turned_ref[real, atoms : 2 * atoms] + im * turned_ref[imag, atoms : 2 * atoms]
        return im * g - re * h

    for tile in range(13):
        cc, ss, sc, cs = factors(tile, cx, sx, cy, sy)
        up, down = add(0, tile, cc - ss, sc + cs), add(1, tile, cc + ss, sc - cs)
        if tile < 10:
            sums["x_row"] += up + down
            sums["y"] += (tile + 1.0) * (up - down)
        else:
            sums["x"] += (tile - 2.0) * (up + down)
            sums["y_row"] += up - down
    for core in range(2):
        a, b = late_orders(core, atoms)
        b = b * (1.0 - 2.0 * core)
        late_c, late_s = cos_sin(a * x + b * y)
        for j in range(3):
            rows = slice(8 * j, 8 * j + 8)
            d = add(core, 13 + j, late_c[rows], late_s[rows])
            sums["x"] += a[rows] * d
            sums["y"] += b[rows] * d
    order = lax.broadcasted_iota(jnp.int32, (8, atoms), 0).astype(F32) + 1.0
    down = lambda v: jnp.sum(v, axis=0, keepdims=True)
    energy_ref[...] = 0.25 * down(sums["e"])
    force_ref[0:1, :] = 0.1 * down(sums["x"] + order * sums["x_row"])
    force_ref[1:2, :] = 0.1 * down(sums["y"] + order * sums["y_row"])
    force_ref[2:3, :] = 0.1 * down(sums["z"])


def call(kernel, out_shape, operands, scratch=(), scalar=False):
    vmem = pl.BlockSpec(memory_space=pltpu.VMEM)
    in_specs = [vmem] * operands
    if scalar:
        in_specs = [pl.BlockSpec(memory_space=pltpu.SMEM)] + in_specs
    return pl.pallas_call(
        kernel,
        out_shape=out_shape,
        in_specs=in_specs,
        out_specs=jax.tree.map(lambda _: vmem, out_shape),
        scratch_shapes=list(scratch),
        compiler_params=pltpu.CompilerParams(vmem_limit_bytes=32 * 1024 * 1024),
    )


def per_device(scale, positions, charges, miller):
    atoms = positions.shape[1]
    copies = lax.axis_size("zh")
    shape = lambda *s: jax.ShapeDtypeStruct(s, F32)
    core = lax.axis_index("c").astype(jnp.int32).reshape(1)
    from_root = [(lax.axis_index(axis).astype(jnp.int32) + (4 - at)) % 4 for axis, at in zip(("y", "x"), ROOT)]
    tile = (from_root[0] * 4 + from_root[1]).reshape(1)
    where = core * HALVES + tile * 2 + (lax.axis_index("zl").astype(jnp.int32) & 1)
    rows = lambda a, first: jnp.pad(a, ((first, 16 - first - a.shape[0]), (0, 0)))
    own = rows(charges, 0) + rows(positions, 8) + rows(miller, 11).astype(F32)
    pair = lax.all_gather(own, "c")
    half = [pltpu.VMEM((2 * TILES * ROWS, 6 * atoms), BF16)]
    layer, column = layer_groups(), column_groups()
    part = call(struct_kernel, shape(HALVES, SHARD, LANES), 1, half, scalar=True)(where, pair)
    part = lax.all_to_all(part, AXES, 0, 0, axis_index_groups=layer, tiled=True)
    part = call(collect_kernel, shape(len(column[0]), SHARD, LANES), 1)(part)
    part = lax.all_to_all(part, AXES, 0, 0, axis_index_groups=column, tiled=True)
    weigh = functools.partial(weigh_kernel, scale, copies)
    w = call(weigh, shape(HALVES, SHARD, LANES), 1, scalar=True)(where, part)
    w = lax.all_to_all(w, AXES, 0, 0, axis_index_groups=layer, tiled=True)
    w = lax.all_gather(w, "c")
    wide = [pltpu.VMEM((4 * TILES * ROWS, 2 * atoms), F32)]
    energy, force = call(apply_kernel, (shape(1, atoms), shape(3, atoms)), 2, wide)(own, w)
    return energy.reshape(atoms), force


def solution(mesh):
    fine = Mesh(mesh.devices.reshape(SHAPE), AXES)
    in_specs = (P(None, AXES), P(None, AXES), P(None, "zl"))
    out_specs = (P(AXES), P(None, AXES))

    def run(positions, charges, miller):
        scale = 1.0 / float(positions.shape[1]) ** 0.5
        body = functools.partial(per_device, scale)
        return jax.shard_map(body, mesh=fine, in_specs=in_specs, out_specs=out_specs, check_vma=False)(
            positions, charges, miller
        )

    return run
```

```python
import functools

import jax
import jax.numpy as jnp
import numpy as np
from jax import lax
from jax.experimental import pallas as pl
from jax.experimental.pallas import tpu as pltpu
from jax.sharding import Mesh
from jax.sharding import PartitionSpec as P

TOP = 10
TILES = 16
ROWS = 8
HALVES = 2 * TILES
SHARD = 4
HALF = 176
LANES = 384
COUNT_LANE = 352
SIN = (3.141592640130706, -5.167710083507839, 2.550077523214083, -0.5982912856178239, 0.07765766030006041)
COS = (
    1.0,
    -4.934802137078852,
    4.058709159556494,
    -1.3352120030499017,
    0.23493731380758293,
    -0.02439632432974524,
)
F32 = jnp.float32
BF16 = jnp.bfloat16
SHAPE = (8, 4, 2, 4, 2)
AXES = ("zl", "y", "zh", "x", "c")
ROOT = (2, 2)


def device(z, y, x, c):
    return int(np.arange(512).reshape(SHAPE)[z % 8, y, z // 8, x, c])


def layer_groups():
    chips = [((n // 4 + ROOT[0]) % 4, (n % 4 + ROOT[1]) % 4) for n in range(TILES)]
    return [[device(z + half, y, x, c) for half in (1, 0) for y, x in chips] for z in range(0, 16, 2) for c in (0, 1)]


def column_groups():
    order = [(8 + n // 2 * 2 + 8 * (n % 2)) % 16 for n in range(8)]
    rest = [(half, y, x, c) for half in (0, 1) for y in range(4) for x in range(4) for c in (0, 1)]
    return [[device(z + half, y, x, c) for z in order] for half, y, x, c in rest]


def horner(coefs, u):
    out = jnp.full_like(u, coefs[-1])
    for c in coefs[-2::-1]:
        out = out * u + c
    return out


def cos_sin(turns):
    t = turns - jnp.round(turns)
    u = t * t
    s = t * horner(SIN, u)
    return 1.0 - 2.0 * s * s, 2.0 * s * horner(COS, u)


def late_orders(row, steps):
    third = jnp.where(row >= 6, 2, jnp.where(row >= 3, 1, 0))
    return 8 + (third if steps else row - 3 * third)


def table(coordinate, steps=False):
    r = lax.broadcasted_iota(jnp.int32, (16, coordinate.shape[1]), 0)
    return cos_sin(jnp.where(r < 8, r, late_orders(r - 8, steps)).astype(F32) * coordinate)


def split(x):
    high = x.astype(BF16)
    return high, (x - high.astype(F32)).astype(BF16)


def factors(tile, cx, sx, cy, sy):
    if tile < 11:
        b = (tile + 1) % 11
        rows, at = slice(0, 8), b if b < 8 else 3 * b - 16
        columns = slice(at, at + 1)
    elif tile < 14:
        rows, columns = slice(tile - 3, tile - 2), slice(0, 8)
    elif tile == 14:
        rows, columns = slice(8, 16), slice(8, 16)
    else:
        rows, columns = slice(10, 11), slice(14, 15)
    ca, sa, cb, sb = cx[rows], sx[rows], cy[columns], sy[columns]
    if tile == 15:
        ca, sa = jnp.broadcast_to(ca, (8, ca.shape[1])), jnp.broadcast_to(sa, (8, sa.shape[1]))
    return ca * cb, sa * sb, sa * cb, ca * sb


def z_rows(rows, charges):
    return [rows[n : n + 1] * charges for n in range(TOP + 1)]


def nt(a, b):
    return lax.dot_general(a, b, (((1,), (1,)), ((), ())), preferred_element_type=F32)


def nn(a, b):
    return jnp.dot(a, b, preferred_element_type=F32)


def stack(*parts):
    return jnp.concatenate([p for part in parts for p in part], axis=0)


def struct_kernel(where_ref, atoms_ref, out_ref, pairs_ref):
    core, mine = where_ref[0] // HALVES, where_ref[0] % HALVES // 2
    both = jnp.concatenate([atoms_ref[0], atoms_ref[1]], axis=1)
    lanes = both.shape[1]
    x, z, charges = both[8:9], both[10:11], both[0:8]
    y = both[9:10] * jnp.where(core == 0, 1.0, -1.0)
    cx, sx = table(x)
    cy, sy = table(y, steps=True)
    cz, sz = table(z)

    def keep(rows, value):
        high, low = split(value)
        pairs_ref[rows, 0:lanes] = high
        pairs_ref[rows, lanes : 2 * lanes] = low
        pairs_ref[rows, 2 * lanes : 3 * lanes] = high

    for two in range(TILES // 2):
        real, imag = [], []
        for tile in (2 * two, 2 * two + 1):
            cc, ss, sc, cs = factors(tile, cx, sx, cy, sy)
            real.append(cc - ss)
            imag.append(sc + cs)
        keep(slice(16 * two, 16 * two + 16), stack(real))
        keep(slice(128 + 16 * two, 128 + 16 * two + 16), stack(imag))
    cq = z_rows(cz, charges)
    sq = z_rows(sz, charges)
    high, low = split(stack(cq, sq, [jnp.zeros((256 - HALF, lanes), F32)]))
    sums = nt(pairs_ref[...], jnp.concatenate([high, high, low], axis=1))
    real, imag = sums[0:128], pltpu.roll(sums[128:256], HALF - 128, 1)
    middle = real[:, 128:256] + imag[:, 0:128]
    for n in range(HALVES):
        at = ROWS * (n % TILES) + SHARD * (n // TILES)
        rows = slice(at, at + SHARD)
        out_ref[n, :, 0:128] = real[rows, 0:128]
        out_ref[n, :, 128:256] = middle[rows]
        out_ref[n, :, 256:384] = imag[rows, 128:256]
    listed = [atoms_ref[0, r : r + 1, :].astype(jnp.int32) for r in (11, 12, 13)]
    counts = count_listed((core * TILES + mine) * ROWS, *listed)
    for half in range(2):
        own = out_ref.at[TILES * half + mine, :, 256:384]
        own[...] = own[...] + counts[SHARD * half : SHARD * half + SHARD]


def place_of(a, b):
    core = jnp.where(b < 0, 1, 0)
    b = jnp.abs(b)
    corner = 14 * 8 + a - 8 + 3 * (b - 8)
    late = jnp.where(b <= 7, (a + 3) * 8 + b, corner)
    return core * (TILES * ROWS) + jnp.where(a <= 7, jnp.where(b == 0, 10, b - 1) * 8 + a, late)


def count_listed(place, a, b, c):
    sign = jnp.where((a < 0) | ((a == 0) & (b > 0)), -1, 1)
    a, b, c = a * sign, b * sign, c * sign
    listed = a.shape[1]
    row = place_of(a, b) - place
    pair = (row == lax.broadcasted_iota(jnp.int32, (ROWS, listed), 0)).astype(F32)
    lane = c + (TOP + COUNT_LANE - 256)
    third = (lane == lax.broadcasted_iota(jnp.int32, (128, listed), 0)).astype(F32)
    return nt(pair.astype(BF16), third.astype(BF16))


def collect_kernel(part_ref, out_ref):
    out_ref[...] = jnp.broadcast_to(jnp.sum(part_ref[...], axis=0), out_ref.shape)


def weigh_kernel(scale, copies, where_ref, part_ref, out_ref):
    total = stack([jnp.sum(part_ref[...], axis=0), jnp.zeros((ROWS - SHARD, LANES), F32)])
    tile = where_ref[0] % HALVES // 2
    row = lax.broadcasted_iota(jnp.int32, (ROWS, LANES), 0) + SHARD * (where_ref[0] % 2)
    lane = lax.broadcasted_iota(jnp.int32, (ROWS, LANES), 1)
    inner = jnp.where(lane >= HALF, lane - HALF, lane)
    second = inner >= HALF // 2
    c = jnp.where(second, inner - HALF // 2, inner) >> 3
    late = tile >= 14
    a = jnp.where(tile < 11, row, jnp.where(late, late_orders(row, False), tile - 3))
    b = jnp.where(tile < 10, tile + 1, jnp.where(tile == 10, 0, jnp.where(late, late_orders(row, True), row)))
    a, b = jnp.where(tile == 15, 10, a), jnp.where(tile == 15, 10, b)
    square = jnp.maximum(a * a + b * b + c * c, 1).astype(F32)
    weight = jnp.exp(-0.025 * square) / square * scale
    wide_lane = lax.broadcasted_iota(jnp.int32, (128, LANES), 1)
    wide_inner = jnp.where(wide_lane >= HALF, wide_lane - HALF, wide_lane)
    wide_c = jnp.where(wide_inner >= HALF // 2, wide_inner - HALF // 2, wide_inner) >> 3
    offset = lax.broadcasted_iota(jnp.int32, (128, LANES), 0) - (TOP + COUNT_LANE - 256)
    live = wide_lane < COUNT_LANE
    plus = (live & (offset == wide_c)).astype(F32)
    minus = (live & (offset == -wide_c) & (wide_c > 0)).astype(F32)
    counts = total[:, 256:384].astype(BF16)
    both = nn(counts, (plus + minus).astype(BF16)) * (1.0 / copies)
    differ = nn(counts, (plus - minus).astype(BF16)) * (1.0 / copies)
    near, far = HALF // 2, HALF + HALF // 2
    ahead = jnp.where(second, pltpu.roll(total, LANES - near, 1), pltpu.roll(total, LANES - far, 1))
    behind = jnp.where(second, pltpu.roll(total, far, 1), pltpu.roll(total, near, 1))
    partner = jnp.where(lane < HALF, ahead, behind)
    differ = jnp.where(second == (lane < HALF), differ, -differ)
    out = weight * (both * total + differ * partner)
    out_ref[...] = jnp.broadcast_to(out[0:SHARD], out_ref.shape)


def apply_kernel(atoms_ref, w_ref, energy_ref, force_ref, turned_ref):
    x, y, z, charges = atoms_ref[8:9, :], atoms_ref[9:10, :], atoms_ref[10:11, :], atoms_ref[0:8, :]
    atoms = x.shape[1]
    cx, sx = table(x)
    cy, sy = table(y, steps=True)
    cz, sz = table(z)
    cq = z_rows(cz, charges)
    sq = z_rows(sz, charges)
    dc = [n * sq[n] for n in range(TOP + 1)]
    ds = [-n * cq[n] for n in range(TOP + 1)]
    blank = [jnp.zeros((256 - HALF, atoms), F32)]
    high, low = split(jnp.concatenate([stack(cq, sq, blank), stack(dc, ds, blank)], axis=1))
    w = stack([w_ref[core, n] for core in range(2) for tile in range(TILES) for n in (tile, TILES + tile)])
    w = jnp.concatenate([w[:, 0:256], pltpu.roll(w[:, 128:384], 256 - (HALF - 128), 1)], axis=0)
    w_high, w_low = split(w)
    turned_ref[...] = nn(jnp.concatenate([w_high, w_low, w_high], axis=1), jnp.concatenate([high, high, low], axis=0))
    zero = jnp.zeros((8, atoms), F32)
    sums = {"e": zero, "z": zero, "x": zero, "y": zero, "x_row": zero, "y_row": zero}

    def add(core, tile, re, im):
        at = 8 * (core * TILES + tile)
        real, imag = slice(at, at + 8), slice(at + 2 * TILES * ROWS, at + 2 * TILES * ROWS + 8)
        g, h = turned_ref[real, 0:atoms], turned_ref[imag, 0:atoms]
        sums["e"] += re * g + im * h
        sums["z"] += re * turned_ref[real, atoms : 2 * atoms] + im * turned_ref[imag, atoms : 2 * atoms]
        return im * g - re * h

    order = lax.broadcasted_iota(jnp.int32, (8, atoms), 0)
    for tile in range(TILES):
        cc, ss, sc, cs = factors(tile, cx, sx, cy, sy)
        up = add(0, tile, cc - ss, sc + cs)
        down = add(1, tile, cc + ss, sc - cs) if tile != 10 else jnp.zeros_like(up)
        if tile < 11:
            sums["x_row"] += up + down
            sums["y"] += ((tile + 1.0) % 11.0) * (up - down)
        elif tile < 14:
            sums["x"] += (tile - 3.0) * (up + down)
            sums["y_row"] += up - down
        else:
            late = [late_orders(order, steps).astype(F32) if tile == 14 else 10.0 for steps in (False, True)]
            sums["x"] += late[0] * (up + down)
            sums["y"] += late[1] * (up - down)
    order = order.astype(F32)
    down = lambda v: jnp.sum(v, axis=0, keepdims=True)
    energy_ref[...] = 0.25 * down(sums["e"])
    force_ref[0:1, :] = 0.1 * down(sums["x"] + order * sums["x_row"])
    force_ref[1:2, :] = 0.1 * down(sums["y"] + order * sums["y_row"])
    force_ref[2:3, :] = 0.1 * down(sums["z"])


def call(kernel, out_shape, operands, scratch=(), scalar=False):
    vmem = pl.BlockSpec(memory_space=pltpu.VMEM)
    in_specs = [vmem] * operands
    if scalar:
        in_specs = [pl.BlockSpec(memory_space=pltpu.SMEM)] + in_specs
    return pl.pallas_call(
        kernel,
        out_shape=out_shape,
        in_specs=in_specs,
        out_specs=jax.tree.map(lambda _: vmem, out_shape),
        scratch_shapes=list(scratch),
        compiler_params=pltpu.CompilerParams(vmem_limit_bytes=32 * 1024 * 1024),
    )


def per_device(scale, positions, charges, miller):
    atoms = positions.shape[1]
    copies = lax.axis_size("zh")
    shape = lambda *s: jax.ShapeDtypeStruct(s, F32)
    core = lax.axis_index("c").astype(jnp.int32).reshape(1)
    from_root = [(lax.axis_index(axis).astype(jnp.int32) + (4 - at)) % 4 for axis, at in zip(("y", "x"), ROOT)]
    tile = (from_root[0] * 4 + from_root[1]).reshape(1)
    where = core * HALVES + tile * 2 + 1 - (lax.axis_index("zl").astype(jnp.int32) & 1)
    rows = lambda a, first: jnp.pad(a, ((first, 16 - first - a.shape[0]), (0, 0)))
    own = rows(charges, 0) + rows(positions, 8) + rows(miller, 11).astype(F32)
    pair = lax.all_gather(own, "c")
    half = [pltpu.VMEM((2 * TILES * ROWS, 6 * atoms), BF16)]
    layer, column = layer_groups(), column_groups()
    part = call(struct_kernel, shape(HALVES, SHARD, LANES), 1, half, scalar=True)(where, pair)
    part = lax.all_to_all(part, AXES, 0, 0, axis_index_groups=layer, tiled=True)
    part = call(collect_kernel, shape(len(column[0]), SHARD, LANES), 1)(part)
    part = lax.all_to_all(part, AXES, 0, 0, axis_index_groups=column, tiled=True)
    weigh = functools.partial(weigh_kernel, scale, copies)
    w = call(weigh, shape(HALVES, SHARD, LANES), 1, scalar=True)(where, part)
    w = lax.all_to_all(w, AXES, 0, 0, axis_index_groups=layer, tiled=True)
    w = lax.all_gather(w, "c")
    wide = [pltpu.VMEM((4 * TILES * ROWS, 2 * atoms), F32)]
    energy, force = call(apply_kernel, (shape(1, atoms), shape(3, atoms)), 2, wide)(own, w)
    return energy.reshape(atoms), force


def solution(mesh):
    fine = Mesh(mesh.devices.reshape(SHAPE), AXES)
    in_specs = (P(None, AXES), P(None, AXES), P(None, "zl"))
    out_specs = (P(AXES), P(None, AXES))

    def run(positions, charges, miller):
        scale = 1.0 / float(positions.shape[1]) ** 0.5
        body = functools.partial(per_device, scale)
        return jax.shard_map(body, mesh=fine, in_specs=in_specs, out_specs=out_specs, check_vma=False)(
            positions, charges, miller
        )

    return run
```

```python
import functools

import jax
import jax.numpy as jnp
import numpy as np
from jax import lax
from jax.experimental import pallas as pl
from jax.experimental.pallas import tpu as pltpu
from jax.sharding import Mesh
from jax.sharding import PartitionSpec as P

TOP = 10
TILES = 16
ROWS = 8
HALVES = 2 * TILES
SHARD = 4
HALF = 176
LANES = 384
COUNT_LANE = 352
SIN = (3.141592640130706, -5.167710083507839, 2.550077523214083, -0.5982912856178239, 0.07765766030006041)
COS = (
    1.0,
    -4.934802137078852,
    4.058709159556494,
    -1.3352120030499017,
    0.23493731380758293,
    -0.02439632432974524,
)
F32 = jnp.float32
BF16 = jnp.bfloat16
SHAPE = (8, 4, 2, 4, 2)
AXES = ("zl", "y", "zh", "x", "c")
ROOT = (2, 2)


def device(z, y, x, part):
    z = z % 16
    return int(np.arange(512).reshape(SHAPE)[z % 8, y, z // 8, x, part ^ (z // 8)])


def layer_groups():
    chips = [((n // 4 + ROOT[0]) % 4, (n % 4 + ROOT[1]) % 4) for n in range(TILES)]
    return [[device(z + half, y, x, part) for half in (1, 0) for y, x in chips] for z in range(0, 16, 2) for part in (0, 1)]


def column_groups():
    order = range(8, 24, 2)
    rest = [(half, y, x, part) for half in (0, 1) for y in range(4) for x in range(4) for part in (0, 1)]
    return [[device(z + half, y, x, part) for z in order] for half, y, x, part in rest]


def horner(coefs, u):
    out = jnp.full_like(u, coefs[-1])
    for c in coefs[-2::-1]:
        out = out * u + c
    return out


def cos_sin(turns):
    t = turns - jnp.round(turns)
    u = t * t
    s = t * horner(SIN, u)
    return 1.0 - 2.0 * s * s, 2.0 * s * horner(COS, u)


def late_orders(row, steps):
    third = jnp.where(row >= 6, 2, jnp.where(row >= 3, 1, 0))
    return 8 + (third if steps else row - 3 * third)


def table(coordinate, steps=False):
    r = lax.broadcasted_iota(jnp.int32, (16, coordinate.shape[1]), 0)
    return cos_sin(jnp.where(r < 8, r, late_orders(r - 8, steps)).astype(F32) * coordinate)


def split(x):
    high = x.astype(BF16)
    return high, (x - high.astype(F32)).astype(BF16)


def factors(tile, cx, sx, cy, sy):
    if tile < 11:
        b = (tile + 1) % 11
        rows, at = slice(0, 8), b if b < 8 else 3 * b - 16
        columns = slice(at, at + 1)
    elif tile < 14:
        rows, columns = slice(tile - 3, tile - 2), slice(0, 8)
    elif tile == 14:
        rows, columns = slice(8, 16), slice(8, 16)
    else:
        rows, columns = slice(10, 11), slice(14, 15)
    ca, sa, cb, sb = cx[rows], sx[rows], cy[columns], sy[columns]
    if tile == 15:
        ca, sa = jnp.broadcast_to(ca, (8, ca.shape[1])), jnp.broadcast_to(sa, (8, sa.shape[1]))
    return ca * cb, sa * sb, sa * cb, ca * sb


def z_rows(rows, charges):
    return [rows[n : n + 1] * charges for n in range(TOP + 1)]


def nt(a, b):
    return lax.dot_general(a, b, (((1,), (1,)), ((), ())), preferred_element_type=F32)


def nn(a, b):
    return jnp.dot(a, b, preferred_element_type=F32)


def stack(*parts):
    return jnp.concatenate([p for part in parts for p in part], axis=0)


def struct_kernel(where_ref, atoms_ref, out_ref, pairs_ref):
    core, mine = where_ref[0] // HALVES, where_ref[0] % HALVES // 2
    both = jnp.concatenate([atoms_ref[0], atoms_ref[1]], axis=1)
    lanes = both.shape[1]
    x, z, charges = both[8:9], both[10:11], both[0:8]
    y = both[9:10] * jnp.where(core == 0, 1.0, -1.0)
    cx, sx = table(x)
    cy, sy = table(y, steps=True)
    cz, sz = table(z)

    def keep(rows, value):
        high, low = split(value)
        pairs_ref[rows, 0:lanes] = high
        pairs_ref[rows, lanes : 2 * lanes] = low
        pairs_ref[rows, 2 * lanes : 3 * lanes] = high

    for two in range(TILES // 2):
        real, imag = [], []
        for tile in (2 * two, 2 * two + 1):
            cc, ss, sc, cs = factors(tile, cx, sx, cy, sy)
            real.append(cc - ss)
            imag.append(sc + cs)
        keep(slice(16 * two, 16 * two + 16), stack(real))
        keep(slice(128 + 16 * two, 128 + 16 * two + 16), stack(imag))
    cq = z_rows(cz, charges)
    sq = z_rows(sz, charges)
    high, low = split(stack(cq, sq, [jnp.zeros((256 - HALF, lanes), F32)]))
    sums = nt(pairs_ref[...], jnp.concatenate([high, high, low], axis=1))
    real, imag = sums[0:128], pltpu.roll(sums[128:256], HALF - 128, 1)
    middle = real[:, 128:256] + imag[:, 0:128]
    for n in range(HALVES):
        at = ROWS * (n % TILES) + SHARD * (n // TILES)
        rows = slice(at, at + SHARD)
        out_ref[n, :, 0:128] = real[rows, 0:128]
        out_ref[n, :, 128:256] = middle[rows]
        out_ref[n, :, 256:384] = imag[rows, 128:256]
    listed = [atoms_ref[0, r : r + 1, :].astype(jnp.int32) for r in (11, 12, 13)]
    counts = count_listed((core * TILES + mine) * ROWS, *listed)
    for half in range(2):
        own = out_ref.at[TILES * half + mine, :, 256:384]
        own[...] = own[...] + counts[SHARD * half : SHARD * half + SHARD]


def place_of(a, b):
    core = jnp.where(b < 0, 1, 0)
    b = jnp.abs(b)
    corner = 14 * 8 + a - 8 + 3 * (b - 8)
    late = jnp.where(b <= 7, (a + 3) * 8 + b, corner)
    return core * (TILES * ROWS) + jnp.where(a <= 7, jnp.where(b == 0, 10, b - 1) * 8 + a, late)


def count_listed(place, a, b, c):
    sign = jnp.where((a < 0) | ((a == 0) & (b > 0)), -1, 1)
    a, b, c = a * sign, b * sign, c * sign
    listed = a.shape[1]
    row = place_of(a, b) - place
    pair = (row == lax.broadcasted_iota(jnp.int32, (ROWS, listed), 0)).astype(F32)
    lane = c + (TOP + COUNT_LANE - 256)
    third = (lane == lax.broadcasted_iota(jnp.int32, (128, listed), 0)).astype(F32)
    return nt(pair.astype(BF16), third.astype(BF16))


def collect_kernel(part_ref, out_ref):
    out_ref[...] = jnp.broadcast_to(jnp.sum(part_ref[...], axis=0), out_ref.shape)


def weigh_kernel(scale, copies, where_ref, part_ref, out_ref):
    total = stack([jnp.sum(part_ref[...], axis=0), jnp.zeros((ROWS - SHARD, LANES), F32)])
    tile = where_ref[0] % HALVES // 2
    row = lax.broadcasted_iota(jnp.int32, (ROWS, LANES), 0) + SHARD * (where_ref[0] % 2)
    lane = lax.broadcasted_iota(jnp.int32, (ROWS, LANES), 1)
    inner = jnp.where(lane >= HALF, lane - HALF, lane)
    second = inner >= HALF // 2
    c = jnp.where(second, inner - HALF // 2, inner) >> 3
    late = tile >= 14
    a = jnp.where(tile < 11, row, jnp.where(late, late_orders(row, False), tile - 3))
    b = jnp.where(tile < 10, tile + 1, jnp.where(tile == 10, 0, jnp.where(late, late_orders(row, True), row)))
    a, b = jnp.where(tile == 15, 10, a), jnp.where(tile == 15, 10, b)
    square = jnp.maximum(a * a + b * b + c * c, 1).astype(F32)
    weight = jnp.exp(-0.025 * square) / square * scale
    wide_lane = lax.broadcasted_iota(jnp.int32, (128, LANES), 1)
    wide_inner = jnp.where(wide_lane >= HALF, wide_lane - HALF, wide_lane)
    wide_c = jnp.where(wide_inner >= HALF // 2, wide_inner - HALF // 2, wide_inner) >> 3
    offset = lax.broadcasted_iota(jnp.int32, (128, LANES), 0) - (TOP + COUNT_LANE - 256)
    live = wide_lane < COUNT_LANE
    plus = (live & (offset == wide_c)).astype(F32)
    minus = (live & (offset == -wide_c) & (wide_c > 0)).astype(F32)
    counts = total[:, 256:384].astype(BF16)
    both = nn(counts, (plus + minus).astype(BF16)) * (1.0 / copies)
    differ = nn(counts, (plus - minus).astype(BF16)) * (1.0 / copies)
    near, far = HALF // 2, HALF + HALF // 2
    ahead = jnp.where(second, pltpu.roll(total, LANES - near, 1), pltpu.roll(total, LANES - far, 1))
    behind = jnp.where(second, pltpu.roll(total, far, 1), pltpu.roll(total, near, 1))
    partner = jnp.where(lane < HALF, ahead, behind)
    differ = jnp.where(second == (lane < HALF), differ, -differ)
    out = weight * (both * total + differ * partner)
    out_ref[...] = jnp.broadcast_to(out[0:SHARD], out_ref.shape)


def apply_kernel(cross_ref, atoms_ref, w_ref, energy_ref, force_ref, turned_ref):
    x, y, z, charges = atoms_ref[8:9, :], atoms_ref[9:10, :], atoms_ref[10:11, :], atoms_ref[0:8, :]
    atoms = x.shape[1]
    cx, sx = table(x)
    cy, sy = table(y, steps=True)
    cz, sz = table(z)
    cq = z_rows(cz, charges)
    sq = z_rows(sz, charges)
    dc = [n * sq[n] for n in range(TOP + 1)]
    ds = [-n * cq[n] for n in range(TOP + 1)]
    blank = [jnp.zeros((256 - HALF, atoms), F32)]
    high, low = split(jnp.concatenate([stack(cq, sq, blank), stack(dc, ds, blank)], axis=1))
    cross = cross_ref[0]
    w = stack([w_ref[core, n] for core in (cross, 1 - cross) for tile in range(TILES) for n in (tile, TILES + tile)])
    w = jnp.concatenate([w[:, 0:256], pltpu.roll(w[:, 128:384], 256 - (HALF - 128), 1)], axis=0)
    w_high, w_low = split(w)
    turned_ref[...] = nn(jnp.concatenate([w_high, w_low, w_high], axis=1), jnp.concatenate([high, high, low], axis=0))
    zero = jnp.zeros((8, atoms), F32)
    sums = {"e": zero, "z": zero, "x": zero, "y": zero, "x_row": zero, "y_row": zero}

    def add(core, tile, re, im):
        at = 8 * (core * TILES + tile)
        real, imag = slice(at, at + 8), slice(at + 2 * TILES * ROWS, at + 2 * TILES * ROWS + 8)
        g, h = turned_ref[real, 0:atoms], turned_ref[imag, 0:atoms]
        sums["e"] += re * g + im * h
        sums["z"] += re * turned_ref[real, atoms : 2 * atoms] + im * turned_ref[imag, atoms : 2 * atoms]
        return im * g - re * h

    order = lax.broadcasted_iota(jnp.int32, (8, atoms), 0)
    for tile in range(TILES):
        cc, ss, sc, cs = factors(tile, cx, sx, cy, sy)
        up = add(0, tile, cc - ss, sc + cs)
        down = add(1, tile, cc + ss, sc - cs) if tile != 10 else jnp.zeros_like(up)
        if tile < 11:
            sums["x_row"] += up + down
            sums["y"] += ((tile + 1.0) % 11.0) * (up - down)
        elif tile < 14:
            sums["x"] += (tile - 3.0) * (up + down)
            sums["y_row"] += up - down
        else:
            late = [late_orders(order, steps).astype(F32) if tile == 14 else 10.0 for steps in (False, True)]
            sums["x"] += late[0] * (up + down)
            sums["y"] += late[1] * (up - down)
    order = order.astype(F32)
    down = lambda v: jnp.sum(v, axis=0, keepdims=True)
    energy_ref[...] = 0.25 * down(sums["e"])
    force_ref[0:1, :] = 0.1 * down(sums["x"] + order * sums["x_row"])
    force_ref[1:2, :] = 0.1 * down(sums["y"] + order * sums["y_row"])
    force_ref[2:3, :] = 0.1 * down(sums["z"])


def call(kernel, out_shape, operands, scratch=(), scalar=False):
    vmem = pl.BlockSpec(memory_space=pltpu.VMEM)
    in_specs = [vmem] * operands
    if scalar:
        in_specs = [pl.BlockSpec(memory_space=pltpu.SMEM)] + in_specs
    return pl.pallas_call(
        kernel,
        out_shape=out_shape,
        in_specs=in_specs,
        out_specs=jax.tree.map(lambda _: vmem, out_shape),
        scratch_shapes=list(scratch),
        compiler_params=pltpu.CompilerParams(vmem_limit_bytes=32 * 1024 * 1024),
    )


def per_device(scale, positions, charges, miller):
    atoms = positions.shape[1]
    copies = lax.axis_size("zh")
    shape = lambda *s: jax.ShapeDtypeStruct(s, F32)
    cross = lax.axis_index("zh").astype(jnp.int32).reshape(1)
    part_of = lax.axis_index("c").astype(jnp.int32).reshape(1) ^ cross
    from_root = [(lax.axis_index(axis).astype(jnp.int32) + (4 - at)) % 4 for axis, at in zip(("y", "x"), ROOT)]
    tile = (from_root[0] * 4 + from_root[1]).reshape(1)
    where = part_of * HALVES + tile * 2 + 1 - (lax.axis_index("zl").astype(jnp.int32) & 1)
    rows = lambda a, first: jnp.pad(a, ((first, 16 - first - a.shape[0]), (0, 0)))
    own = rows(charges, 0) + rows(positions, 8) + rows(miller, 11).astype(F32)
    pair = lax.all_gather(own, "c")
    half = [pltpu.VMEM((2 * TILES * ROWS, 6 * atoms), BF16)]
    layer, column = layer_groups(), column_groups()
    part = call(struct_kernel, shape(HALVES, SHARD, LANES), 1, half, scalar=True)(where, pair)
    part = lax.all_to_all(part, AXES, 0, 0, axis_index_groups=layer, tiled=True)
    part = call(collect_kernel, shape(len(column[0]), SHARD, LANES), 1)(part)
    part = lax.all_to_all(part, AXES, 0, 0, axis_index_groups=column, tiled=True)
    weigh = functools.partial(weigh_kernel, scale, copies)
    w = call(weigh, shape(HALVES, SHARD, LANES), 1, scalar=True)(where, part)
    w = lax.all_to_all(w, AXES, 0, 0, axis_index_groups=layer, tiled=True)
    w = lax.all_gather(w, "c")
    wide = [pltpu.VMEM((4 * TILES * ROWS, 2 * atoms), F32)]
    energy, force = call(apply_kernel, (shape(1, atoms), shape(3, atoms)), 2, wide, scalar=True)(cross, own, w)
    return energy.reshape(atoms), force


def solution(mesh):
    fine = Mesh(mesh.devices.reshape(SHAPE), AXES)
    in_specs = (P(None, AXES), P(None, AXES), P(None, "zl"))
    out_specs = (P(AXES), P(None, AXES))

    def run(positions, charges, miller):
        scale = 1.0 / float(positions.shape[1]) ** 0.5
        body = functools.partial(per_device, scale)
        return jax.shard_map(body, mesh=fine, in_specs=in_specs, out_specs=out_specs, check_vma=False)(
            positions, charges, miller
        )

    return run
```

```python
import functools

import jax
import jax.numpy as jnp
import numpy as np
from jax import lax
from jax.experimental import pallas as pl
from jax.experimental.pallas import tpu as pltpu
from jax.sharding import Mesh
from jax.sharding import PartitionSpec as P

TOP = 10
TILES = 16
ROWS = 8
HALVES = 2 * TILES
SHARD = 4
HALF = 176
LANES = 384
COUNT_LANE = 352
SIN = (3.141592640130706, -5.167710083507839, 2.550077523214083, -0.5982912856178239, 0.07765766030006041)
COS = (
    1.0,
    -4.934802137078852,
    4.058709159556494,
    -1.3352120030499017,
    0.23493731380758293,
    -0.02439632432974524,
)
F32 = jnp.float32
BF16 = jnp.bfloat16
SHAPE = (8, 4, 2, 4, 2)
AXES = ("zl", "y", "zh", "x", "c")
ROOT = (2, 2)


def device(z, y, x, part):
    z = z % 16
    return int(np.arange(512).reshape(SHAPE)[z % 8, y, z // 8, x, part ^ (z // 8)])


def layer_groups():
    chips = [((n // 4 + ROOT[0]) % 4, (n % 4 + ROOT[1]) % 4) for n in range(TILES)]
    return [[device(z + half, y, x, part) for half in (1, 0) for y, x in chips] for z in range(0, 16, 2) for part in (0, 1)]


def column_groups():
    order = range(8, 24, 2)
    rest = [(half, y, x, part) for half in (0, 1) for y in range(4) for x in range(4) for part in (0, 1)]
    return [[device(z + half, y, x, part) for z in order] for half, y, x, part in rest]


def horner(coefs, u):
    out = jnp.full_like(u, coefs[-1])
    for c in coefs[-2::-1]:
        out = out * u + c
    return out


def cos_sin(turns):
    t = turns - jnp.round(turns)
    u = t * t
    s = t * horner(SIN, u)
    return 1.0 - 2.0 * s * s, 2.0 * s * horner(COS, u)


def late_orders(row, steps):
    third = jnp.where(row >= 6, 2, jnp.where(row >= 3, 1, 0))
    return 8 + (third if steps else row - 3 * third)


def table(coordinate, steps=False):
    r = lax.broadcasted_iota(jnp.int32, (16, coordinate.shape[1]), 0)
    return cos_sin(jnp.where(r < 8, r, late_orders(r - 8, steps)).astype(F32) * coordinate)


def split(x):
    high = x.astype(BF16)
    return high, (x - high.astype(F32)).astype(BF16)


def factors(tile, cx, sx, cy, sy):
    if tile < 11:
        b = (tile + 1) % 11
        rows, at = slice(0, 8), b if b < 8 else 3 * b - 16
        columns = slice(at, at + 1)
    elif tile < 14:
        rows, columns = slice(tile - 3, tile - 2), slice(0, 8)
    elif tile == 14:
        rows, columns = slice(8, 16), slice(8, 16)
    else:
        rows, columns = slice(10, 11), slice(14, 15)
    ca, sa, cb, sb = cx[rows], sx[rows], cy[columns], sy[columns]
    if tile == 15:
        ca, sa = jnp.broadcast_to(ca, (8, ca.shape[1])), jnp.broadcast_to(sa, (8, sa.shape[1]))
    return ca * cb, sa * sb, sa * cb, ca * sb


def z_rows(rows, charges):
    return [rows[n : n + 1] * charges for n in range(TOP + 1)]


def nt(a, b):
    return lax.dot_general(a, b, (((1,), (1,)), ((), ())), preferred_element_type=F32)


def nn(a, b):
    return jnp.dot(a, b, preferred_element_type=F32)


def stack(*parts):
    return jnp.concatenate([p for part in parts for p in part], axis=0)


def struct_kernel(where_ref, atoms_ref, out_ref, pairs_ref):
    core, mine = where_ref[0] // HALVES, where_ref[0] % HALVES // 2
    sums = 0.0
    for n in range(2):
        own = atoms_ref[n]
        lanes = own.shape[1]
        first = 3 * lanes * n
        x, z, charges = own[8:9], own[10:11], own[0:8]
        y = own[9:10] * jnp.where(core == 0, 1.0, -1.0)
        cx, sx = table(x)
        cy, sy = table(y, steps=True)
        cz, sz = table(z)

        def keep(rows, value):
            high, low = split(value)
            pairs_ref[rows, first : first + lanes] = high
            pairs_ref[rows, first + lanes : first + 2 * lanes] = low
            pairs_ref[rows, first + 2 * lanes : first + 3 * lanes] = high

        for two in range(TILES // 2):
            real, imag = [], []
            for tile in (2 * two, 2 * two + 1):
                cc, ss, sc, cs = factors(tile, cx, sx, cy, sy)
                real.append(cc - ss)
                imag.append(sc + cs)
            keep(slice(16 * two, 16 * two + 16), stack(real))
            keep(slice(128 + 16 * two, 128 + 16 * two + 16), stack(imag))
        cq = z_rows(cz, charges)
        sq = z_rows(sz, charges)
        high, low = split(stack(cq, sq, [jnp.zeros((256 - HALF, lanes), F32)]))
        sums += nt(pairs_ref[:, first : first + 3 * lanes], jnp.concatenate([high, high, low], axis=1))
    real, imag = sums[0:128], pltpu.roll(sums[128:256], HALF - 128, 1)
    middle = real[:, 128:256] + imag[:, 0:128]
    for n in range(HALVES):
        at = ROWS * (n % TILES) + SHARD * (n // TILES)
        rows = slice(at, at + SHARD)
        out_ref[n, :, 0:128] = real[rows, 0:128]
        out_ref[n, :, 128:256] = middle[rows]
        out_ref[n, :, 256:384] = imag[rows, 128:256]
    listed = [atoms_ref[0, r : r + 1, :].astype(jnp.int32) for r in (11, 12, 13)]
    counts = count_listed((core * TILES + mine) * ROWS, *listed)
    for half in range(2):
        own = out_ref.at[TILES * half + mine, :, 256:384]
        own[...] = own[...] + counts[SHARD * half : SHARD * half + SHARD]


def place_of(a, b):
    core = jnp.where(b < 0, 1, 0)
    b = jnp.abs(b)
    corner = 14 * 8 + a - 8 + 3 * (b - 8)
    late = jnp.where(b <= 7, (a + 3) * 8 + b, corner)
    return core * (TILES * ROWS) + jnp.where(a <= 7, jnp.where(b == 0, 10, b - 1) * 8 + a, late)


def count_listed(place, a, b, c):
    sign = jnp.where((a < 0) | ((a == 0) & (b > 0)), -1, 1)
    a, b, c = a * sign, b * sign, c * sign
    listed = a.shape[1]
    row = place_of(a, b) - place
    pair = (row == lax.broadcasted_iota(jnp.int32, (ROWS, listed), 0)).astype(F32)
    lane = c + (TOP + COUNT_LANE - 256)
    third = (lane == lax.broadcasted_iota(jnp.int32, (128, listed), 0)).astype(F32)
    return nt(pair.astype(BF16), third.astype(BF16))


def collect_kernel(part_ref, out_ref):
    out_ref[...] = jnp.broadcast_to(jnp.sum(part_ref[...], axis=0), out_ref.shape)


def weigh_kernel(scale, copies, where_ref, part_ref, out_ref):
    total = stack([jnp.sum(part_ref[...], axis=0), jnp.zeros((ROWS - SHARD, LANES), F32)])
    tile = where_ref[0] % HALVES // 2
    row = lax.broadcasted_iota(jnp.int32, (ROWS, LANES), 0) + SHARD * (where_ref[0] % 2)
    lane = lax.broadcasted_iota(jnp.int32, (ROWS, LANES), 1)
    inner = jnp.where(lane >= HALF, lane - HALF, lane)
    second = inner >= HALF // 2
    c = jnp.where(second, inner - HALF // 2, inner) >> 3
    late = tile >= 14
    a = jnp.where(tile < 11, row, jnp.where(late, late_orders(row, False), tile - 3))
    b = jnp.where(tile < 10, tile + 1, jnp.where(tile == 10, 0, jnp.where(late, late_orders(row, True), row)))
    a, b = jnp.where(tile == 15, 10, a), jnp.where(tile == 15, 10, b)
    square = jnp.maximum(a * a + b * b + c * c, 1).astype(F32)
    weight = jnp.exp(-0.025 * square) / square * scale
    wide_lane = lax.broadcasted_iota(jnp.int32, (32, LANES), 1)
    wide_inner = jnp.where(wide_lane >= HALF, wide_lane - HALF, wide_lane)
    wide_c = jnp.where(wide_inner >= HALF // 2, wide_inner - HALF // 2, wide_inner) >> 3
    offset = lax.broadcasted_iota(jnp.int32, (32, LANES), 0) - TOP
    live = wide_lane < COUNT_LANE
    plus = (live & (offset == wide_c)).astype(F32)
    minus = (live & (offset == -wide_c) & (wide_c > 0)).astype(F32)
    counts = pltpu.roll(total[:, 256:384], 32, 1)[:, 0:32].astype(BF16)
    both = nn(counts, (plus + minus).astype(BF16)) * (1.0 / copies)
    differ = nn(counts, (plus - minus).astype(BF16)) * (1.0 / copies)
    near, far = HALF // 2, HALF + HALF // 2
    ahead = jnp.where(second, pltpu.roll(total, LANES - near, 1), pltpu.roll(total, LANES - far, 1))
    behind = jnp.where(second, pltpu.roll(total, far, 1), pltpu.roll(total, near, 1))
    partner = jnp.where(lane < HALF, ahead, behind)
    differ = jnp.where(second == (lane < HALF), differ, -differ)
    out = weight * (both * total + differ * partner)
    out_ref[...] = jnp.broadcast_to(out[0:SHARD], out_ref.shape)


def apply_kernel(cross_ref, atoms_ref, w_ref, energy_ref, force_ref, turned_ref):
    x, y, z, charges = atoms_ref[8:9, :], atoms_ref[9:10, :], atoms_ref[10:11, :], atoms_ref[0:8, :]
    atoms = x.shape[1]
    cx, sx = table(x)
    cy, sy = table(y, steps=True)
    cz, sz = table(z)
    cq = z_rows(cz, charges)
    sq = z_rows(sz, charges)
    dc = [n * sq[n] for n in range(TOP + 1)]
    ds = [-n * cq[n] for n in range(TOP + 1)]
    blank = [jnp.zeros((256 - HALF, atoms), F32)]
    high, low = split(jnp.concatenate([stack(cq, sq, blank), stack(dc, ds, blank)], axis=1))
    cross = cross_ref[0]
    w = stack([w_ref[core, n] for core in (cross, 1 - cross) for tile in range(TILES) for n in (tile, TILES + tile)])
    w = jnp.concatenate([w[:, 0:256], pltpu.roll(w[:, 128:384], 256 - (HALF - 128), 1)], axis=0)
    w_high, w_low = split(w)
    turned_ref[...] = nn(jnp.concatenate([w_high, w_low, w_high], axis=1), jnp.concatenate([high, high, low], axis=0))
    zero = jnp.zeros((8, atoms), F32)
    sums = {"e": zero, "z": zero, "x": zero, "y": zero, "x_row": zero, "y_row": zero}

    def add(core, tile, re, im):
        at = 8 * (core * TILES + tile)
        real, imag = slice(at, at + 8), slice(at + 2 * TILES * ROWS, at + 2 * TILES * ROWS + 8)
        g, h = turned_ref[real, 0:atoms], turned_ref[imag, 0:atoms]
        sums["e"] += re * g + im * h
        sums["z"] += re * turned_ref[real, atoms : 2 * atoms] + im * turned_ref[imag, atoms : 2 * atoms]
        return im * g - re * h

    order = lax.broadcasted_iota(jnp.int32, (8, atoms), 0)
    for tile in range(TILES):
        cc, ss, sc, cs = factors(tile, cx, sx, cy, sy)
        up = add(0, tile, cc - ss, sc + cs)
        down = add(1, tile, cc + ss, sc - cs) if tile != 10 else jnp.zeros_like(up)
        if tile < 11:
            sums["x_row"] += up + down
            sums["y"] += ((tile + 1.0) % 11.0) * (up - down)
        elif tile < 14:
            sums["x"] += (tile - 3.0) * (up + down)
            sums["y_row"] += up - down
        else:
            late = [late_orders(order, steps).astype(F32) if tile == 14 else 10.0 for steps in (False, True)]
            sums["x"] += late[0] * (up + down)
            sums["y"] += late[1] * (up - down)
    order = order.astype(F32)
    down = lambda v: jnp.sum(v, axis=0, keepdims=True)
    energy_ref[...] = 0.25 * down(sums["e"])
    force_ref[0:1, :] = 0.1 * down(sums["x"] + order * sums["x_row"])
    force_ref[1:2, :] = 0.1 * down(sums["y"] + order * sums["y_row"])
    force_ref[2:3, :] = 0.1 * down(sums["z"])


def call(kernel, out_shape, operands, scratch=(), scalar=False):
    vmem = pl.BlockSpec(memory_space=pltpu.VMEM)
    in_specs = [vmem] * operands
    if scalar:
        in_specs = [pl.BlockSpec(memory_space=pltpu.SMEM)] + in_specs
    return pl.pallas_call(
        kernel,
        out_shape=out_shape,
        in_specs=in_specs,
        out_specs=jax.tree.map(lambda _: vmem, out_shape),
        scratch_shapes=list(scratch),
        compiler_params=pltpu.CompilerParams(vmem_limit_bytes=32 * 1024 * 1024),
    )


def per_device(scale, positions, charges, miller):
    atoms = positions.shape[1]
    copies = lax.axis_size("zh")
    shape = lambda *s: jax.ShapeDtypeStruct(s, F32)
    cross = lax.axis_index("zh").astype(jnp.int32).reshape(1)
    part_of = lax.axis_index("c").astype(jnp.int32).reshape(1) ^ cross
    from_root = [(lax.axis_index(axis).astype(jnp.int32) + (4 - at)) % 4 for axis, at in zip(("y", "x"), ROOT)]
    tile = (from_root[0] * 4 + from_root[1]).reshape(1)
    where = part_of * HALVES + tile * 2 + 1 - (lax.axis_index("zl").astype(jnp.int32) & 1)
    rows = lambda a, first: jnp.pad(a, ((first, 16 - first - a.shape[0]), (0, 0)))
    own = rows(charges, 0) + rows(positions, 8) + rows(miller, 11).astype(F32)
    pair = lax.all_gather(own, "c")
    half = [pltpu.VMEM((2 * TILES * ROWS, 6 * atoms), BF16)]
    layer, column = layer_groups(), column_groups()
    part = call(struct_kernel, shape(HALVES, SHARD, LANES), 1, half, scalar=True)(where, pair)
    part = lax.all_to_all(part, AXES, 0, 0, axis_index_groups=layer, tiled=True)
    part = call(collect_kernel, shape(len(column[0]), SHARD, LANES), 1)(part)
    part = lax.all_to_all(part, AXES, 0, 0, axis_index_groups=column, tiled=True)
    weigh = functools.partial(weigh_kernel, scale, copies)
    w = call(weigh, shape(HALVES, SHARD, LANES), 1, scalar=True)(where, part)
    w = lax.all_to_all(w, AXES, 0, 0, axis_index_groups=layer, tiled=True)
    w = lax.all_gather(w, "c")
    wide = [pltpu.VMEM((4 * TILES * ROWS, 2 * atoms), F32)]
    energy, force = call(apply_kernel, (shape(1, atoms), shape(3, atoms)), 2, wide, scalar=True)(cross, own, w)
    return energy.reshape(atoms), force


def solution(mesh):
    fine = Mesh(mesh.devices.reshape(SHAPE), AXES)
    in_specs = (P(None, AXES), P(None, AXES), P(None, "zl"))
    out_specs = (P(AXES), P(None, AXES))

    def run(positions, charges, miller):
        scale = 1.0 / float(positions.shape[1]) ** 0.5
        body = functools.partial(per_device, scale)
        return jax.shard_map(body, mesh=fine, in_specs=in_specs, out_specs=out_specs, check_vma=False)(
            positions, charges, miller
        )

    return run
```

```python
import functools

import jax
import jax.numpy as jnp
import numpy as np
from jax import lax
from jax.experimental import pallas as pl
from jax.experimental.pallas import tpu as pltpu
from jax.sharding import Mesh
from jax.sharding import PartitionSpec as P

TOP = 10
TILES = 16
ROWS = 8
HALVES = 2 * TILES
SHARD = 4
HALF = 176
LANES = 384
COUNT_LANE = 352
SIN = (3.141592640130706, -5.167710083507839, 2.550077523214083, -0.5982912856178239, 0.07765766030006041)
COS = (
    1.0,
    -4.934802137078852,
    4.058709159556494,
    -1.3352120030499017,
    0.23493731380758293,
    -0.02439632432974524,
)
F32 = jnp.float32
BF16 = jnp.bfloat16
SHAPE = (8, 4, 2, 4, 2)
AXES = ("zl", "y", "zh", "x", "c")
ROOT = (2, 2)


def device(z, y, x, part):
    z = z % 16
    return int(np.arange(512).reshape(SHAPE)[z % 8, y, z // 8, x, part ^ (1 - z // 8)])


def layer_groups():
    chips = [((n // 4 + ROOT[0]) % 4, (n % 4 + ROOT[1]) % 4) for n in range(TILES)]
    return [[device(z + half, y, x, part) for half in (1, 0) for y, x in chips] for z in range(0, 16, 2) for part in (0, 1)]


def column_groups():
    order = range(8, 24, 2)
    rest = [(half, y, x, part) for half in (0, 1) for y in range(4) for x in range(4) for part in (0, 1)]
    return [[device(z + half, y, x, part) for z in order] for half, y, x, part in rest]


def horner(coefs, u):
    out = jnp.full_like(u, coefs[-1])
    for c in coefs[-2::-1]:
        out = out * u + c
    return out


def cos_sin(turns):
    t = turns - jnp.round(turns)
    u = t * t
    s = t * horner(SIN, u)
    return 1.0 - 2.0 * s * s, 2.0 * s * horner(COS, u)


def late_orders(row, steps):
    third = jnp.where(row >= 6, 2, jnp.where(row >= 3, 1, 0))
    return 8 + (third if steps else row - 3 * third)


def table(coordinate, steps=False):
    r = lax.broadcasted_iota(jnp.int32, (16, coordinate.shape[1]), 0)
    return cos_sin(jnp.where(r < 8, r, late_orders(r - 8, steps)).astype(F32) * coordinate)


def split(x):
    high = x.astype(BF16)
    return high, (x - high.astype(F32)).astype(BF16)


def factors(tile, cx, sx, cy, sy):
    if tile < 11:
        b = (tile + 1) % 11
        rows, at = slice(0, 8), b if b < 8 else 3 * b - 16
        columns = slice(at, at + 1)
    elif tile < 14:
        rows, columns = slice(tile - 3, tile - 2), slice(0, 8)
    elif tile == 14:
        rows, columns = slice(8, 16), slice(8, 16)
    else:
        rows, columns = slice(10, 11), slice(14, 15)
    ca, sa, cb, sb = cx[rows], sx[rows], cy[columns], sy[columns]
    if tile == 15:
        ca, sa = jnp.broadcast_to(ca, (8, ca.shape[1])), jnp.broadcast_to(sa, (8, sa.shape[1]))
    return ca * cb, sa * sb, sa * cb, ca * sb


def z_rows(rows, charges):
    return [rows[n : n + 1] * charges for n in range(TOP + 1)]


def nt(a, b):
    return lax.dot_general(a, b, (((1,), (1,)), ((), ())), preferred_element_type=F32)


def nn(a, b):
    return jnp.dot(a, b, preferred_element_type=F32)


def stack(*parts):
    return jnp.concatenate([p for part in parts for p in part], axis=0)


def struct_kernel(where_ref, atoms_ref, out_ref, pairs_ref):
    core, mine = where_ref[0] // HALVES, where_ref[0] % HALVES // 2
    sums = 0.0
    for n in range(2):
        own = atoms_ref[n]
        lanes = own.shape[1]
        first = 3 * lanes * n
        x, z, charges = own[8:9], own[10:11], own[0:8]
        y = own[9:10] * jnp.where(core == 0, 1.0, -1.0)
        cx, sx = table(x)
        cy, sy = table(y, steps=True)
        cz, sz = table(z)

        def keep(rows, value):
            high, low = split(value)
            pairs_ref[rows, first : first + lanes] = high
            pairs_ref[rows, first + lanes : first + 2 * lanes] = low
            pairs_ref[rows, first + 2 * lanes : first + 3 * lanes] = high

        for two in range(TILES // 2):
            real, imag = [], []
            for tile in (2 * two, 2 * two + 1):
                cc, ss, sc, cs = factors(tile, cx, sx, cy, sy)
                real.append(cc - ss)
                imag.append(sc + cs)
            keep(slice(16 * two, 16 * two + 16), stack(real))
            keep(slice(128 + 16 * two, 128 + 16 * two + 16), stack(imag))
        cq = z_rows(cz, charges)
        sq = z_rows(sz, charges)
        high, low = split(stack(cq, sq, [jnp.zeros((256 - HALF, lanes), F32)]))
        sums += nt(pairs_ref[:, first : first + 3 * lanes], jnp.concatenate([high, high, low], axis=1))
    real, imag = sums[0:128], pltpu.roll(sums[128:256], HALF - 128, 1)
    middle = real[:, 128:256] + imag[:, 0:128]
    for n in range(HALVES):
        at = ROWS * (n % TILES) + SHARD * (n // TILES)
        rows = slice(at, at + SHARD)
        out_ref[n, :, 0:128] = real[rows, 0:128]
        out_ref[n, :, 128:256] = middle[rows]
        out_ref[n, :, 256:384] = imag[rows, 128:256]
    listed = [atoms_ref[0, r : r + 1, :].astype(jnp.int32) for r in (11, 12, 13)]
    counts = count_listed((core * TILES + mine) * ROWS, *listed)
    for half in range(2):
        own = out_ref.at[TILES * half + mine, :, 256:384]
        own[...] = own[...] + counts[SHARD * half : SHARD * half + SHARD]


def place_of(a, b):
    core = jnp.where(b < 0, 1, 0)
    b = jnp.abs(b)
    corner = 14 * 8 + a - 8 + 3 * (b - 8)
    late = jnp.where(b <= 7, (a + 3) * 8 + b, corner)
    return core * (TILES * ROWS) + jnp.where(a <= 7, jnp.where(b == 0, 10, b - 1) * 8 + a, late)


def count_listed(place, a, b, c):
    sign = jnp.where((a < 0) | ((a == 0) & (b > 0)), -1, 1)
    a, b, c = a * sign, b * sign, c * sign
    listed = a.shape[1]
    row = place_of(a, b) - place
    pair = (row == lax.broadcasted_iota(jnp.int32, (ROWS, listed), 0)).astype(F32)
    lane = c + (TOP + COUNT_LANE - 256)
    third = (lane == lax.broadcasted_iota(jnp.int32, (128, listed), 0)).astype(F32)
    return nt(pair.astype(BF16), third.astype(BF16))


def collect_kernel(part_ref, out_ref):
    out_ref[...] = jnp.broadcast_to(jnp.sum(part_ref[...], axis=0), out_ref.shape)


def weigh_kernel(scale, copies, where_ref, part_ref, out_ref):
    total = stack([jnp.sum(part_ref[...], axis=0), jnp.zeros((ROWS - SHARD, LANES), F32)])
    tile = where_ref[0] % HALVES // 2
    row = lax.broadcasted_iota(jnp.int32, (ROWS, LANES), 0) + SHARD * (where_ref[0] % 2)
    lane = lax.broadcasted_iota(jnp.int32, (ROWS, LANES), 1)
    inner = jnp.where(lane >= HALF, lane - HALF, lane)
    second = inner >= HALF // 2
    c = jnp.where(second, inner - HALF // 2, inner) >> 3
    late = tile >= 14
    a = jnp.where(tile < 11, row, jnp.where(late, late_orders(row, False), tile - 3))
    b = jnp.where(tile < 10, tile + 1, jnp.where(tile == 10, 0, jnp.where(late, late_orders(row, True), row)))
    a, b = jnp.where(tile == 15, 10, a), jnp.where(tile == 15, 10, b)
    square = jnp.maximum(a * a + b * b + c * c, 1).astype(F32)
    weight = jnp.exp(-0.025 * square) / square * scale
    wide_lane = lax.broadcasted_iota(jnp.int32, (32, LANES), 1)
    wide_inner = jnp.where(wide_lane >= HALF, wide_lane - HALF, wide_lane)
    wide_c = jnp.where(wide_inner >= HALF // 2, wide_inner - HALF // 2, wide_inner) >> 3
    offset = lax.broadcasted_iota(jnp.int32, (32, LANES), 0) - TOP
    live = wide_lane < COUNT_LANE
    plus = (live & (offset == wide_c)).astype(F32)
    minus = (live & (offset == -wide_c) & (wide_c > 0)).astype(F32)
    counts = pltpu.roll(total[:, 256:384], 32, 1)[:, 0:32].astype(BF16)
    both = nn(counts, (plus + minus).astype(BF16)) * (1.0 / copies)
    differ = nn(counts, (plus - minus).astype(BF16)) * (1.0 / copies)
    near, far = HALF // 2, HALF + HALF // 2
    ahead = jnp.where(second, pltpu.roll(total, LANES - near, 1), pltpu.roll(total, LANES - far, 1))
    behind = jnp.where(second, pltpu.roll(total, far, 1), pltpu.roll(total, near, 1))
    partner = jnp.where(lane < HALF, ahead, behind)
    differ = jnp.where(second == (lane < HALF), differ, -differ)
    out = weight * (both * total + differ * partner)
    out_ref[...] = jnp.broadcast_to(out[0:SHARD], out_ref.shape)


def apply_kernel(cross_ref, atoms_ref, w_ref, energy_ref, force_ref, turned_ref):
    x, y, z, charges = atoms_ref[8:9, :], atoms_ref[9:10, :], atoms_ref[10:11, :], atoms_ref[0:8, :]
    atoms = x.shape[1]
    cx, sx = table(x)
    cy, sy = table(y, steps=True)
    cz, sz = table(z)
    cq = z_rows(cz, charges)
    sq = z_rows(sz, charges)
    dc = [n * sq[n] for n in range(TOP + 1)]
    ds = [-n * cq[n] for n in range(TOP + 1)]
    blank = [jnp.zeros((256 - HALF, atoms), F32)]
    high, low = split(jnp.concatenate([stack(cq, sq, blank), stack(dc, ds, blank)], axis=1))
    cross = cross_ref[0]
    w = stack([w_ref[core, n] for core in (cross, 1 - cross) for tile in range(TILES) for n in (tile, TILES + tile)])
    w = jnp.concatenate([w[:, 0:256], pltpu.roll(w[:, 128:384], 256 - (HALF - 128), 1)], axis=0)
    w_high, w_low = split(w)
    turned_ref[...] = nn(jnp.concatenate([w_high, w_low, w_high], axis=1), jnp.concatenate([high, high, low], axis=0))
    zero = jnp.zeros((8, atoms), F32)
    sums = {"e": zero, "z": zero, "x": zero, "y": zero, "x_row": zero, "y_row": zero}

    def add(core, tile, re, im):
        at = 8 * (core * TILES + tile)
        real, imag = slice(at, at + 8), slice(at + 2 * TILES * ROWS, at + 2 * TILES * ROWS + 8)
        g, h = turned_ref[real, 0:atoms], turned_ref[imag, 0:atoms]
        sums["e"] += re * g + im * h
        sums["z"] += re * turned_ref[real, atoms : 2 * atoms] + im * turned_ref[imag, atoms : 2 * atoms]
        return im * g - re * h

    order = lax.broadcasted_iota(jnp.int32, (8, atoms), 0)
    for tile in range(TILES):
        cc, ss, sc, cs = factors(tile, cx, sx, cy, sy)
        up = add(0, tile, cc - ss, sc + cs)
        down = add(1, tile, cc + ss, sc - cs) if tile != 10 else jnp.zeros_like(up)
        if tile < 11:
            sums["x_row"] += up + down
            sums["y"] += ((tile + 1.0) % 11.0) * (up - down)
        elif tile < 14:
            sums["x"] += (tile - 3.0) * (up + down)
            sums["y_row"] += up - down
        else:
            late = [late_orders(order, steps).astype(F32) if tile == 14 else 10.0 for steps in (False, True)]
            sums["x"] += late[0] * (up + down)
            sums["y"] += late[1] * (up - down)
    order = order.astype(F32)
    down = lambda v: jnp.sum(v, axis=0, keepdims=True)
    energy_ref[...] = 0.25 * down(sums["e"])
    force_ref[0:1, :] = 0.1 * down(sums["x"] + order * sums["x_row"])
    force_ref[1:2, :] = 0.1 * down(sums["y"] + order * sums["y_row"])
    force_ref[2:3, :] = 0.1 * down(sums["z"])


def call(kernel, out_shape, operands, scratch=(), scalar=False):
    vmem = pl.BlockSpec(memory_space=pltpu.VMEM)
    in_specs = [vmem] * operands
    if scalar:
        in_specs = [pl.BlockSpec(memory_space=pltpu.SMEM)] + in_specs
    return pl.pallas_call(
        kernel,
        out_shape=out_shape,
        in_specs=in_specs,
        out_specs=jax.tree.map(lambda _: vmem, out_shape),
        scratch_shapes=list(scratch),
        compiler_params=pltpu.CompilerParams(vmem_limit_bytes=32 * 1024 * 1024),
    )


def per_device(scale, positions, charges, miller):
    atoms = positions.shape[1]
    copies = lax.axis_size("zh")
    shape = lambda *s: jax.ShapeDtypeStruct(s, F32)
    cross = 1 - lax.axis_index("zh").astype(jnp.int32).reshape(1)
    part_of = lax.axis_index("c").astype(jnp.int32).reshape(1) ^ cross
    from_root = [(lax.axis_index(axis).astype(jnp.int32) + (4 - at)) % 4 for axis, at in zip(("y", "x"), ROOT)]
    tile = (from_root[0] * 4 + from_root[1]).reshape(1)
    where = part_of * HALVES + tile * 2 + 1 - (lax.axis_index("zl").astype(jnp.int32) & 1)
    rows = lambda a, first: jnp.pad(a, ((first, 16 - first - a.shape[0]), (0, 0)))
    own = rows(charges, 0) + rows(positions, 8) + rows(miller, 11).astype(F32)
    pair = lax.all_gather(own, "c")
    half = [pltpu.VMEM((2 * TILES * ROWS, 6 * atoms), BF16)]
    layer, column = layer_groups(), column_groups()
    part = call(struct_kernel, shape(HALVES, SHARD, LANES), 1, half, scalar=True)(where, pair)
    part = lax.all_to_all(part, AXES, 0, 0, axis_index_groups=layer, tiled=True)
    part = call(collect_kernel, shape(len(column[0]), SHARD, LANES), 1)(part)
    part = lax.all_to_all(part, AXES, 0, 0, axis_index_groups=column, tiled=True)
    weigh = functools.partial(weigh_kernel, scale, copies)
    w = call(weigh, shape(HALVES, SHARD, LANES), 1, scalar=True)(where, part)
    w = lax.all_to_all(w, AXES, 0, 0, axis_index_groups=layer, tiled=True)
    w = lax.all_gather(w, "c")
    wide = [pltpu.VMEM((4 * TILES * ROWS, 2 * atoms), F32)]
    energy, force = call(apply_kernel, (shape(1, atoms), shape(3, atoms)), 2, wide, scalar=True)(cross, own, w)
    return energy.reshape(atoms), force


def solution(mesh):
    fine = Mesh(mesh.devices.reshape(SHAPE), AXES)
    in_specs = (P(None, AXES), P(None, AXES), P(None, "zl"))
    out_specs = (P(AXES), P(None, AXES))

    def run(positions, charges, miller):
        scale = 1.0 / float(positions.shape[1]) ** 0.5
        body = functools.partial(per_device, scale)
        return jax.shard_map(body, mesh=fine, in_specs=in_specs, out_specs=out_specs, check_vma=False)(
            positions, charges, miller
        )

    return run
```

```python
import functools

import jax
import jax.numpy as jnp
import numpy as np
from jax import lax
from jax.experimental import pallas as pl
from jax.experimental.pallas import tpu as pltpu
from jax.sharding import Mesh
from jax.sharding import PartitionSpec as P

TOP = 10
TILES = 16
ROWS = 8
HALVES = 2 * TILES
SHARD = 4
HALF = 176
LANES = 384
COUNT_LANE = 352
SIN = (3.141592640130706, -5.167710083507839, 2.550077523214083, -0.5982912856178239, 0.07765766030006041)
COS = (0.9999999532476084, -4.934792830619647, 4.058411352862679, -1.3318765680811553, 0.21968961109773877)
F32 = jnp.float32
BF16 = jnp.bfloat16
SHAPE = (8, 4, 2, 4, 2)
AXES = ("zl", "y", "zh", "x", "c")
ROOT = (2, 2)


def device(z, y, x, part):
    z = z % 16
    return int(np.arange(512).reshape(SHAPE)[z % 8, y, z // 8, x, part ^ (1 - z // 8)])


def layer_groups():
    chips = [((n // 4 + ROOT[0]) % 4, (n % 4 + ROOT[1]) % 4) for n in range(TILES)]
    return [[device(z + half, y, x, part) for half in (1, 0) for y, x in chips] for z in range(0, 16, 2) for part in (0, 1)]


def column_groups():
    order = range(8, 24, 2)
    rest = [(half, y, x, part) for half in (0, 1) for y in range(4) for x in range(4) for part in (0, 1)]
    return [[device(z + half, y, x, part) for z in order] for half, y, x, part in rest]


def horner(coefs, u):
    out = jnp.full_like(u, coefs[-1])
    for c in coefs[-2::-1]:
        out = out * u + c
    return out


def cos_sin(turns):
    t = turns - jnp.round(turns)
    u = t * t
    s = t * horner(SIN, u)
    return 1.0 - 2.0 * s * s, 2.0 * s * horner(COS, u)


def late_orders(row, steps):
    third = jnp.where(row >= 6, 2, jnp.where(row >= 3, 1, 0))
    return 8 + (third if steps else row - 3 * third)


def table(coordinate, steps=False):
    r = lax.broadcasted_iota(jnp.int32, (16, coordinate.shape[1]), 0)
    return cos_sin(jnp.where(r < 8, r, late_orders(r - 8, steps)).astype(F32) * coordinate)


def split(x):
    high = x.astype(BF16)
    return high, (x - high.astype(F32)).astype(BF16)


def factors(tile, cx, sx, cy, sy):
    if tile < 11:
        b = (tile + 1) % 11
        rows, at = slice(0, 8), b if b < 8 else 3 * b - 16
        columns = slice(at, at + 1)
    elif tile < 14:
        rows, columns = slice(tile - 3, tile - 2), slice(0, 8)
    elif tile == 14:
        rows, columns = slice(8, 16), slice(8, 16)
    else:
        rows, columns = slice(10, 11), slice(14, 15)
    ca, sa, cb, sb = cx[rows], sx[rows], cy[columns], sy[columns]
    if tile == 15:
        ca, sa = jnp.broadcast_to(ca, (8, ca.shape[1])), jnp.broadcast_to(sa, (8, sa.shape[1]))
    return ca * cb, sa * sb, sa * cb, ca * sb


def z_rows(rows, charges):
    return [rows[n : n + 1] * charges for n in range(TOP + 1)]


def nt(a, b):
    return lax.dot_general(a, b, (((1,), (1,)), ((), ())), preferred_element_type=F32)


def nn(a, b):
    return jnp.dot(a, b, preferred_element_type=F32)


def stack(*parts):
    return jnp.concatenate([p for part in parts for p in part], axis=0)


def struct_kernel(where_ref, atoms_ref, out_ref, pairs_ref):
    core, mine = where_ref[0] // HALVES, where_ref[0] % HALVES // 2
    sums = 0.0
    for n in range(2):
        own = atoms_ref[n]
        lanes = own.shape[1]
        first = 3 * lanes * n
        x, z, charges = own[8:9], own[10:11], own[0:8]
        y = own[9:10] * jnp.where(core == 0, 1.0, -1.0)
        cx, sx = table(x)
        cy, sy = table(y, steps=True)
        cz, sz = table(z)

        def keep(rows, value):
            high, low = split(value)
            pairs_ref[rows, first : first + lanes] = high
            pairs_ref[rows, first + lanes : first + 2 * lanes] = low
            pairs_ref[rows, first + 2 * lanes : first + 3 * lanes] = high

        for two in range(TILES // 2):
            real, imag = [], []
            for tile in (2 * two, 2 * two + 1):
                cc, ss, sc, cs = factors(tile, cx, sx, cy, sy)
                real.append(cc - ss)
                imag.append(sc + cs)
            keep(slice(16 * two, 16 * two + 16), stack(real))
            keep(slice(128 + 16 * two, 128 + 16 * two + 16), stack(imag))
        cq = z_rows(cz, charges)
        sq = z_rows(sz, charges)
        high, low = split(stack(cq, sq, [jnp.zeros((256 - HALF, lanes), F32)]))
        sums += nt(pairs_ref[:, first : first + 3 * lanes], jnp.concatenate([high, high, low], axis=1))
    real, imag = sums[0:128], pltpu.roll(sums[128:256], HALF - 128, 1)
    middle = real[:, 128:256] + imag[:, 0:128]
    for n in range(HALVES):
        at = ROWS * (n % TILES) + SHARD * (n // TILES)
        rows = slice(at, at + SHARD)
        out_ref[n, :, 0:128] = real[rows, 0:128]
        out_ref[n, :, 128:256] = middle[rows]
        out_ref[n, :, 256:384] = imag[rows, 128:256]
    listed = [atoms_ref[0, r : r + 1, :].astype(jnp.int32) for r in (11, 12, 13)]
    counts = count_listed((core * TILES + mine) * ROWS, *listed)
    for half in range(2):
        own = out_ref.at[TILES * half + mine, :, 256:384]
        own[...] = own[...] + counts[SHARD * half : SHARD * half + SHARD]


def place_of(a, b):
    core = jnp.where(b < 0, 1, 0)
    b = jnp.abs(b)
    corner = 14 * 8 + a - 8 + 3 * (b - 8)
    late = jnp.where(b <= 7, (a + 3) * 8 + b, corner)
    return core * (TILES * ROWS) + jnp.where(a <= 7, jnp.where(b == 0, 10, b - 1) * 8 + a, late)


def count_listed(place, a, b, c):
    sign = jnp.where((a < 0) | ((a == 0) & (b > 0)), -1, 1)
    a, b, c = a * sign, b * sign, c * sign
    listed = a.shape[1]
    row = place_of(a, b) - place
    pair = (row == lax.broadcasted_iota(jnp.int32, (ROWS, listed), 0)).astype(F32)
    lane = c + (TOP + COUNT_LANE - 256)
    third = (lane == lax.broadcasted_iota(jnp.int32, (128, listed), 0)).astype(F32)
    return nt(pair.astype(BF16), third.astype(BF16))


def collect_kernel(part_ref, out_ref):
    out_ref[...] = jnp.broadcast_to(jnp.sum(part_ref[...], axis=0), out_ref.shape)


def weigh_kernel(scale, copies, where_ref, part_ref, out_ref):
    total = stack([jnp.sum(part_ref[...], axis=0), jnp.zeros((ROWS - SHARD, LANES), F32)])
    tile = where_ref[0] % HALVES // 2
    row = lax.broadcasted_iota(jnp.int32, (ROWS, LANES), 0) + SHARD * (where_ref[0] % 2)
    lane = lax.broadcasted_iota(jnp.int32, (ROWS, LANES), 1)
    inner = jnp.where(lane >= HALF, lane - HALF, lane)
    second = inner >= HALF // 2
    c = jnp.where(second, inner - HALF // 2, inner) >> 3
    late = tile >= 14
    a = jnp.where(tile < 11, row, jnp.where(late, late_orders(row, False), tile - 3))
    b = jnp.where(tile < 10, tile + 1, jnp.where(tile == 10, 0, jnp.where(late, late_orders(row, True), row)))
    a, b = jnp.where(tile == 15, 10, a), jnp.where(tile == 15, 10, b)
    square = jnp.maximum(a * a + b * b + c * c, 1).astype(F32)
    weight = jnp.exp(-0.025 * square) / square * scale
    wide_lane = lax.broadcasted_iota(jnp.int32, (32, LANES), 1)
    wide_inner = jnp.where(wide_lane >= HALF, wide_lane - HALF, wide_lane)
    wide_c = jnp.where(wide_inner >= HALF // 2, wide_inner - HALF // 2, wide_inner) >> 3
    offset = lax.broadcasted_iota(jnp.int32, (32, LANES), 0) - TOP
    live = wide_lane < COUNT_LANE
    plus = (live & (offset == wide_c)).astype(F32)
    minus = (live & (offset == -wide_c) & (wide_c > 0)).astype(F32)
    counts = pltpu.roll(total[:, 256:384], 32, 1)[:, 0:32].astype(BF16)
    both = nn(counts, (plus + minus).astype(BF16)) * (1.0 / copies)
    differ = nn(counts, (plus - minus).astype(BF16)) * (1.0 / copies)
    near, far = HALF // 2, HALF + HALF // 2
    ahead = jnp.where(second, pltpu.roll(total, LANES - near, 1), pltpu.roll(total, LANES - far, 1))
    behind = jnp.where(second, pltpu.roll(total, far, 1), pltpu.roll(total, near, 1))
    partner = jnp.where(lane < HALF, ahead, behind)
    differ = jnp.where(second == (lane < HALF), differ, -differ)
    out = weight * (both * total + differ * partner)
    out_ref[...] = jnp.broadcast_to(out[0:SHARD], out_ref.shape)


def apply_kernel(cross_ref, atoms_ref, w_ref, energy_ref, force_ref, turned_ref):
    x, y, z, charges = atoms_ref[8:9, :], atoms_ref[9:10, :], atoms_ref[10:11, :], atoms_ref[0:8, :]
    atoms = x.shape[1]
    cx, sx = table(x)
    cy, sy = table(y, steps=True)
    cz, sz = table(z)
    cq = z_rows(cz, charges)
    sq = z_rows(sz, charges)
    dc = [n * sq[n] for n in range(TOP + 1)]
    ds = [-n * cq[n] for n in range(TOP + 1)]
    blank = [jnp.zeros((256 - HALF, atoms), F32)]
    high, low = split(jnp.concatenate([stack(cq, sq, blank), stack(dc, ds, blank)], axis=1))
    cross = cross_ref[0]
    w = stack([w_ref[core, n] for core in (cross, 1 - cross) for tile in range(TILES) for n in (tile, TILES + tile)])
    w = jnp.concatenate([w[:, 0:256], pltpu.roll(w[:, 128:384], 256 - (HALF - 128), 1)], axis=0)
    w_high, w_low = split(w)
    turned_ref[...] = nn(jnp.concatenate([w_high, w_low, w_high], axis=1), jnp.concatenate([high, high, low], axis=0))
    zero = jnp.zeros((8, atoms), F32)
    sums = {"e": zero, "z": zero, "x": zero, "y": zero, "x_row": zero, "y_row": zero}

    def add(core, tile, re, im):
        at = 8 * (core * TILES + tile)
        real, imag = slice(at, at + 8), slice(at + 2 * TILES * ROWS, at + 2 * TILES * ROWS + 8)
        g, h = turned_ref[real, 0:atoms], turned_ref[imag, 0:atoms]
        sums["e"] += re * g + im * h
        sums["z"] += re * turned_ref[real, atoms : 2 * atoms] + im * turned_ref[imag, atoms : 2 * atoms]
        return im * g - re * h

    order = lax.broadcasted_iota(jnp.int32, (8, atoms), 0)
    for tile in range(TILES):
        cc, ss, sc, cs = factors(tile, cx, sx, cy, sy)
        up = add(0, tile, cc - ss, sc + cs)
        down = add(1, tile, cc + ss, sc - cs) if tile != 10 else jnp.zeros_like(up)
        if tile < 11:
            sums["x_row"] += up + down
            sums["y"] += ((tile + 1.0) % 11.0) * (up - down)
        elif tile < 14:
            sums["x"] += (tile - 3.0) * (up + down)
            sums["y_row"] += up - down
        else:
            late = [late_orders(order, steps).astype(F32) if tile == 14 else 10.0 for steps in (False, True)]
            sums["x"] += late[0] * (up + down)
            sums["y"] += late[1] * (up - down)
    order = order.astype(F32)
    down = lambda v: jnp.sum(v, axis=0, keepdims=True)
    energy_ref[...] = 0.25 * down(sums["e"])
    force_ref[0:1, :] = 0.1 * down(sums["x"] + order * sums["x_row"])
    force_ref[1:2, :] = 0.1 * down(sums["y"] + order * sums["y_row"])
    force_ref[2:3, :] = 0.1 * down(sums["z"])


def call(kernel, out_shape, operands, scratch=(), scalar=False):
    vmem = pl.BlockSpec(memory_space=pltpu.VMEM)
    in_specs = [vmem] * operands
    if scalar:
        in_specs = [pl.BlockSpec(memory_space=pltpu.SMEM)] + in_specs
    return pl.pallas_call(
        kernel,
        out_shape=out_shape,
        in_specs=in_specs,
        out_specs=jax.tree.map(lambda _: vmem, out_shape),
        scratch_shapes=list(scratch),
        compiler_params=pltpu.CompilerParams(vmem_limit_bytes=32 * 1024 * 1024),
    )


def per_device(scale, positions, charges, miller):
    atoms = positions.shape[1]
    copies = lax.axis_size("zh")
    shape = lambda *s: jax.ShapeDtypeStruct(s, F32)
    cross = 1 - lax.axis_index("zh").astype(jnp.int32).reshape(1)
    part_of = lax.axis_index("c").astype(jnp.int32).reshape(1) ^ cross
    from_root = [(lax.axis_index(axis).astype(jnp.int32) + (4 - at)) % 4 for axis, at in zip(("y", "x"), ROOT)]
    tile = (from_root[0] * 4 + from_root[1]).reshape(1)
    where = part_of * HALVES + tile * 2 + 1 - (lax.axis_index("zl").astype(jnp.int32) & 1)
    rows = lambda a, first: jnp.pad(a, ((first, 16 - first - a.shape[0]), (0, 0)))
    own = rows(charges, 0) + rows(positions, 8) + rows(miller, 11).astype(F32)
    pair = lax.all_gather(own, "c")
    half = [pltpu.VMEM((2 * TILES * ROWS, 6 * atoms), BF16)]
    layer, column = layer_groups(), column_groups()
    part = call(struct_kernel, shape(HALVES, SHARD, LANES), 1, half, scalar=True)(where, pair)
    part = lax.all_to_all(part, AXES, 0, 0, axis_index_groups=layer, tiled=True)
    part = call(collect_kernel, shape(len(column[0]), SHARD, LANES), 1)(part)
    part = lax.all_to_all(part, AXES, 0, 0, axis_index_groups=column, tiled=True)
    weigh = functools.partial(weigh_kernel, scale, copies)
    w = call(weigh, shape(HALVES, SHARD, LANES), 1, scalar=True)(where, part)
    w = lax.all_to_all(w, AXES, 0, 0, axis_index_groups=layer, tiled=True)
    w = lax.all_gather(w, "c")
    wide = [pltpu.VMEM((4 * TILES * ROWS, 2 * atoms), F32)]
    energy, force = call(apply_kernel, (shape(1, atoms), shape(3, atoms)), 2, wide, scalar=True)(cross, own, w)
    return energy.reshape(atoms), force


def solution(mesh):
    fine = Mesh(mesh.devices.reshape(SHAPE), AXES)
    in_specs = (P(None, AXES), P(None, AXES), P(None, "zl"))
    out_specs = (P(AXES), P(None, AXES))

    def run(positions, charges, miller):
        scale = 1.0 / float(positions.shape[1]) ** 0.5
        body = functools.partial(per_device, scale)
        return jax.shard_map(body, mesh=fine, in_specs=in_specs, out_specs=out_specs, check_vma=False)(
            positions, charges, miller
        )

    return run
```
